256 devices in a mesh: row: 16 (over y, x_lo, core), col: 16 (over z, x_hi).
Axes of the slice: x: 4 (x_hi: 2, x_lo: 2; x = x_hi * 2 + x_lo), y: 4, z: 8, core: 2. Of those that a mesh axis runs over, the one named last changes fastest.
Arguments:
- density: float32 [128, 64, 1024], P('col', 'row'), may hold values from 0.3 to 3
- velocity: float32 [3, 128, 64, 1024], P(None, 'col', 'row'), may hold values from -2 to 2
- pressure: float32 [128, 64, 1024], P('col', 'row'), may hold values from 0.3 to 3
Outputs:
- state: float32 [5, 128, 64, 1024], P(None, 'col', 'row')
The draws below stay inside these ranges and needn't reach their ends.
All inputs are finite; a program needn't handle non-finite values.
Results may differ from the reference program's by a relative error of at most 0.0003.
Values sent between devices are 32-bit elements; how exact they have to be, the bound alone decides.
No kernel may reach another device: no remote copies, remote signals or barrier semaphores. Data moves between devices by JAX's collectives and lax.ppermute only.
A program may use at most 64 MiB of HBM per device.

```python
import math
import jax
import jax.numpy as jnp
from jax import lax

NX = 1024
RIEMANN_ITERS = 3
NY = 64
NZ = 128


def levels(own_key, extent, pieces, least, top_value):
    gain = 1.0
    for axis_at, parts in pieces:
        draws = jax.random.uniform(jax.random.fold_in(jax.random.fold_in(own_key, 6), axis_at), (parts,), jnp.float32, least / len(pieces), top_value / len(pieces))
        gain = gain * jnp.repeat(jnp.exp(draws), extent[axis_at] // parts).reshape((-1,) + (1,) * (len(extent) - 1 - axis_at))
    return gain


def noise(key, extent, spread, most, shards=(), kind=jnp.bfloat16):
    drawn = spread * jax.random.normal(key, extent, jnp.float32)
    if shards:
        drawn = drawn * levels(key, extent, shards, -0.22, 0.18)
    return jnp.clip(drawn, -most, most).astype(kind)


def setup_inputs(seed: int = 0) -> dict:
    keys = jax.random.split(jax.random.key(seed), 4)
    density = jnp.clip(jnp.exp(math.log(3.0) - 2.3025851 * jax.random.uniform(keys[0], (NZ, NY, NX), jnp.float32) ** levels(keys[0], (NZ, NY, NX), ((0, 16), (1, 16)), -0.2, 0.2)), 0.3, 3.0)
    velocity = noise(keys[1], (3, NZ, NY, NX), 0.5, 2.0, ((1, 16), (2, 16)), jnp.float32)
    pressure = jnp.clip(jnp.exp(math.log(3.0) - 2.3025851 * jax.random.uniform(keys[2], (NZ, NY, NX), jnp.float32) ** levels(keys[2], (NZ, NY, NX), ((0, 16), (1, 16)), -0.2, 0.2)), 0.3, 3.0)
    return {"density": density, "velocity": velocity, "pressure": pressure}


GAMMA = 1.4
GM1 = 0.4
SHOCK = (GAMMA + 1.0) / (2.0 * GAMMA)
DTDX = 0.03
PRESSURE_FLOOR = 0.05
STAR_FLOOR = 0.1

def shifted(values, offset, axis):
    return jnp.roll(values, -offset, axis=axis)

def limited(values, axis):
    nearby = shifted(values, 1, axis)
    face = 7.0 / 12.0 * (values + nearby) - 1.0 / 12.0 * (shifted(values, -1, axis) + shifted(values, 2, axis))
    face = jnp.clip(face, jnp.minimum(values, nearby), jnp.maximum(values, nearby))
    right_delta = face - values
    left_delta = shifted(face, -1, axis) - values
    right_limit = jnp.clip(right_delta, -2.0 * jnp.abs(left_delta), 2.0 * jnp.abs(left_delta))
    left_limit = jnp.clip(left_delta, -2.0 * jnp.abs(right_delta), 2.0 * jnp.abs(right_delta))
    return (values + right_limit, shifted(values + left_limit, 1, axis))

def riemann(left_state, right_state):
    dens_left, vel_left, tan_left, cross_left, pres_left = [left_state[index] for index in range(5)]
    dens_right, vel_right, tan_right, cross_right, pres_right = [right_state[index] for index in range(5)]
    sound_left = jnp.sqrt(GAMMA * pres_left * dens_left)
    sound_right = jnp.sqrt(GAMMA * pres_right * dens_right)
    jump = vel_left - vel_right
    floor_star = STAR_FLOOR * jnp.minimum(pres_left, pres_right)

    def combine_star(wave_left, wave_right):
        star = (wave_right * pres_left + wave_left * pres_right + wave_left * wave_right * jump) / (wave_left + wave_right)
        return jnp.maximum(star, floor_star)

    def waves(star_pressure):
        wave_left = sound_left * jnp.sqrt(1.0 + SHOCK * (star_pressure / pres_left - 1.0))
        wave_right = sound_right * jnp.sqrt(1.0 + SHOCK * (star_pressure / pres_right - 1.0))
        return (wave_left, wave_right)
    star_pressure = combine_star(sound_left, sound_right)
    for count in range(RIEMANN_ITERS):
        wave_left, wave_right = waves(star_pressure)
        star_pressure = combine_star(wave_left, wave_right)
    wave_left, wave_right = waves(star_pressure)
    star_velocity = (wave_left * vel_left + wave_right * vel_right + pres_left - pres_right) / (wave_left + wave_right)
    upwind = star_velocity > 0.0
    dens_up = jnp.where(upwind, dens_left, dens_right)
    tan_up = jnp.where(upwind, tan_left, tan_right)
    cross_up = jnp.where(upwind, cross_left, cross_right)
    pres_up = jnp.where(upwind, pres_left, pres_right)
    mass_flux = dens_up * star_velocity
    energy_up = pres_up / GM1 + 0.5 * dens_up * (star_velocity * star_velocity + tan_up * tan_up + cross_up * cross_up)
    return jnp.stack([mass_flux, mass_flux * star_velocity + star_pressure, mass_flux * tan_up, mass_flux * cross_up, star_velocity * (energy_up + star_pressure)])

def sweep_line(state, axis, normal):
    component = {1: (1, 2, 3), 2: (2, 1, 3), 3: (3, 1, 2)}[normal]
    density = state[0]
    velocity_list = [state[index] / density for index in component]
    kinetic = 0.5 * density * (velocity_list[0] ** 2 + velocity_list[1] ** 2 + velocity_list[2] ** 2)
    pressure = jnp.maximum(GM1 * (state[4] - kinetic), PRESSURE_FLOOR)
    primitive = jnp.stack([density] + velocity_list + [pressure])
    left_state, right_state = limited(primitive, axis)
    fluxes = riemann(left_state, right_state)
    change = DTDX * (fluxes - shifted(fluxes, -1, axis))
    updated = [None] * 5
    updated[0] = state[0] - change[0]
    for place in range(3):
        updated[component[place]] = state[component[place]] - change[1 + place]
    updated[4] = state[4] - change[4]
    return jnp.stack(updated)

def initial_state(density, velocity, pressure):
    kinetic = 0.5 * density * lax.optimization_barrier(jnp.sum(velocity * velocity, axis=0))
    return jnp.concatenate([density[None], density[None] * velocity, (pressure / GM1 + kinetic)[None]], axis=0)

def reference(density, velocity, pressure):
    state = initial_state(density, velocity, pressure)
    planes = jnp.moveaxis(state, 1, 0)
    planes = lax.map(lambda plane: sweep_line(sweep_line(plane, 2, 1), 1, 2), planes)
    state = jnp.moveaxis(planes, 0, 1)
    lines = jnp.moveaxis(state, 2, 0)
    lines = lax.map(lambda plane: sweep_line(plane, 1, 3), lines)
    return jnp.moveaxis(lines, 0, 2)
```

```python
import jax
import jax.numpy as jnp
from jax import lax
from jax.experimental import pallas as pl
from jax.experimental.pallas import tpu as pltpu
from jax.sharding import PartitionSpec as P

RIEMANN_ITERS = 3
GAMMA = 1.4
GM1 = 0.4
SHOCK = (GAMMA + 1.0) / (2.0 * GAMMA)
DTDX = 0.03
PRESSURE_FLOOR = 0.05
STAR_FLOOR = 0.1

NX, NY, NZ = 1024, 4, 8
TILES = NX // 128
HALO = 3
F32 = jnp.float32


def face_values(q0, q1, q2, q3):
    face = 7.0 / 12.0 * (q1 + q2) - 1.0 / 12.0 * (q0 + q3)
    return jnp.minimum(jnp.maximum(face, jnp.minimum(q1, q2)), jnp.maximum(q1, q2))


def cell_edges(q, face_left, face_right):
    dr = face_right - q
    dl = face_left - q
    br = 2.0 * jnp.abs(dr)
    bl = 2.0 * jnp.abs(dl)
    right = q + jnp.minimum(jnp.maximum(dr, -bl), bl)
    left = q + jnp.minimum(jnp.maximum(dl, -br), br)
    return left, right


def root(x):
    return x * lax.rsqrt(x)


def inverse(x):
    return 1.0 / x


def riemann(left, right):
    rl, ul, vl, wl, pl_ = left
    rr, ur, vr, wr, pr = right
    al = GAMMA * rl
    ar = GAMMA * rr
    cl = root(al * pl_)
    cr = root(ar * pr)
    jump = ul - ur
    floor = STAR_FLOOR * jnp.minimum(pl_, pr)
    sl = SHOCK * al
    sr = SHOCK * ar
    bl = (1.0 - SHOCK) * al * pl_
    br = (1.0 - SHOCK) * ar * pr

    def star(a, b):
        return jnp.maximum((b * (pl_ + a * jump) + a * pr) * inverse(a + b), floor)

    p = star(cl, cr)
    for _ in range(RIEMANN_ITERS):
        p = star(root(bl + sl * p), root(br + sr * p))
    a = root(bl + sl * p)
    b = root(br + sr * p)
    u = (a * ul + b * ur + (pl_ - pr)) * inverse(a + b)
    up = u > 0.0
    r = jnp.where(up, rl, rr)
    v = jnp.where(up, vl, vr)
    w = jnp.where(up, wl, wr)
    pu = jnp.where(up, pl_, pr)
    m = r * u
    energy = (1.0 / GM1) * pu + 0.5 * r * (u * u + v * v + w * w)
    return m, m * u + p, m * v, m * w, u * (energy + p)


def primitives(state, normal):
    rho = state[0]
    inv = inverse(rho)
    mom = [state[c] for c in normal]
    vel = [m * inv for m in mom]
    kinetic = 0.5 * (mom[0] * vel[0] + mom[1] * vel[1] + mom[2] * vel[2])
    pressure = jnp.maximum(GM1 * (state[4] - kinetic), PRESSURE_FLOOR)
    return [rho] + vel + [pressure]


def line_change(prims, cells):
    left, right = [], []
    for q in prims:
        n = q.shape[0]
        face = face_values(q[0 : n - 3], q[1 : n - 2], q[2 : n - 1], q[3:n])
        lo, hi = cell_edges(q[2 : n - 2], face[: n - 4], face[1:])
        left.append(hi[: cells + 1])
        right.append(lo[1:])
    flux = riemann(left, right)
    return [DTDX * (f[1:] - f[:-1]) for f in flux]


def x_kernel(chunks, d_ref, v_ref, p_ref, *outs):
    per = TILES // chunks
    for y in range(NY):

        def lines(ref, *lead):
            return jnp.concatenate(
                [ref[(*lead, pl.ds(t * NY + y, NZ, stride=TILES * NY), slice(None))] for t in range(TILES)],
                axis=1,
            )

        rho = lines(d_ref)
        vel = [lines(v_ref, c) for c in range(3)]
        pres = lines(p_ref)

        def at(a, k):
            return pltpu.roll(a, (-k) % NX, axis=1) if k else a

        left, right = [], []
        for q in [rho] + vel + [pres]:
            face = face_values(at(q, -1), q, at(q, 1), at(q, 2))
            lo, hi = cell_edges(q, at(face, -1), face)
            left.append(hi)
            right.append(at(lo, 1))
        flux = riemann(left, right)
        change = [DTDX * (f - at(f, -1)) for f in flux]
        kinetic = 0.5 * rho * (vel[0] * vel[0] + vel[1] * vel[1] + vel[2] * vel[2])
        state = [rho] + [rho * u for u in vel] + [(1.0 / GM1) * pres + kinetic]
        for c in range(5):
            new = state[c] - change[c]
            for t in range(TILES):
                s_ref, f_ref, b_ref = outs[3 * (t // per) : 3 * (t // per) + 3]
                piece = new[:, t * 128 : t * 128 + 128]
                s_ref[c, y, t % per] = piece
                if y >= NY - HALO:
                    f_ref[c, y - (NY - HALO), t % per] = piece
                if y < HALO:
                    b_ref[c, y, t % per] = piece


def y_kernel(per, s_ref, lo_ref, hi_ref, t_ref, f_ref, b_ref):
    for t in range(per):
        full = [
            jnp.concatenate([lo_ref[c, :, t], s_ref[c, :, t], hi_ref[c, :, t]], axis=0)
            for c in range(5)
        ]
        change = line_change(primitives(full, (2, 1, 3)), NY)
        for c, k in enumerate((0, 2, 1, 3, 4)):
            new = full[c][HALO : HALO + NY] - change[k]
            for y in range(NY):
                t_ref[c, pl.ds(t * NY + y, NZ, stride=per * NY), :] = new[y]
    width = per * NY
    for c in range(5):
        f_ref[c] = t_ref[c, (NZ - HALO) * width : NZ * width]
        b_ref[c] = t_ref[c, 0 : HALO * width]


def z_kernel(per, t_ref, lo_ref, hi_ref, o_ref):
    width = per * NY
    for r in range(0, width, 8):
        full = [
            jnp.stack(
                [lo_ref[c, z * width + r : z * width + r + 8] for z in range(HALO)]
                + [t_ref[c, z * width + r : z * width + r + 8] for z in range(NZ)]
                + [hi_ref[c, z * width + r : z * width + r + 8] for z in range(HALO)]
            )
            for c in range(5)
        ]
        change = line_change(primitives(full, (3, 1, 2)), NZ)
        for c, k in enumerate((0, 2, 3, 1, 4)):
            new = full[c][HALO : HALO + NZ] - change[k]
            for z in range(NZ):
                o_ref[c, z, r : r + 8] = new[z]


def rows(a):
    lead = a.shape[:-3]
    a = jnp.swapaxes(a.reshape(*lead, NZ, NY, TILES, 128), -2, -3)
    return a.reshape(*lead, NZ * TILES * NY, 128)


def unrows(a):
    a = jnp.swapaxes(a.reshape(5, NZ, TILES, NY, 128), -2, -3)
    return a.reshape(5, NZ, NY, NX)


def shape(*s):
    return jax.ShapeDtypeStruct(s, F32)


CHUNKS = 1


def local(density, velocity, pressure):
    per = TILES // CHUNKS
    width = per * NY
    n = lax.axis_size("row")
    up = [(i, (i + 1) % n) for i in range(n)]
    down = [(i, (i - 1) % n) for i in range(n)]
    x_out = (shape(5, NY, per, NZ, 128), shape(5, HALO, per, NZ, 128), shape(5, HALO, per, NZ, 128))
    parts = pl.pallas_call(
        lambda *refs: x_kernel(CHUNKS, *refs), out_shape=x_out * CHUNKS
    )(rows(density), rows(velocity), rows(pressure))
    z_in = []
    for j in range(CHUNKS):
        s, f, b = parts[3 * j : 3 * j + 3]
        lo = lax.ppermute(f, "row", up)
        hi = lax.ppermute(b, "row", down)
        t, f, b = pl.pallas_call(
            lambda *refs: y_kernel(per, *refs),
            out_shape=(shape(5, NZ * width, 128), shape(5, HALO * width, 128), shape(5, HALO * width, 128)),
        )(s, lo, hi)
        z_in.append((t, lax.ppermute(f, "col", up), lax.ppermute(b, "col", down)))
    assert CHUNKS == 1
    out = pl.pallas_call(
        lambda *refs: z_kernel(per, *refs), out_shape=shape(5, NZ, width, 128)
    )(*z_in[0])
    return unrows(out)


def solution(mesh):
    placed = (P("col", "row", None), P(None, "col", "row", None), P("col", "row", None))
    return jax.shard_map(
        local, mesh=mesh, in_specs=placed, out_specs=P(None, "col", "row", None), check_vma=False
    )
```

```python
import jax
import jax.numpy as jnp
from jax import lax
from jax.experimental import pallas as pl
from jax.experimental.pallas import tpu as pltpu
from jax.sharding import PartitionSpec as P

RIEMANN_ITERS = 3
GAMMA = 1.4
GM1 = 0.4
SHOCK = (GAMMA + 1.0) / (2.0 * GAMMA)
DTDX = 0.03
PRESSURE_FLOOR = 0.05
STAR_FLOOR = 0.1

NX, NY, NZ = 1024, 4, 8
TILES = NX // 128
HALO = 3
F32 = jnp.float32


def face_values(q0, q1, q2, q3):
    face = 7.0 / 12.0 * (q1 + q2) - 1.0 / 12.0 * (q0 + q3)
    return jnp.minimum(jnp.maximum(face, jnp.minimum(q1, q2)), jnp.maximum(q1, q2))


def cell_edges(q, face_left, face_right):
    dr = face_right - q
    dl = face_left - q
    br = 2.0 * jnp.abs(dr)
    bl = 2.0 * jnp.abs(dl)
    right = q + jnp.minimum(jnp.maximum(dr, -bl), bl)
    left = q + jnp.minimum(jnp.maximum(dl, -br), br)
    return left, right


def root(x):
    return x * lax.rsqrt(x)


def inverse(x):
    return 1.0 / x


def riemann(left, right):
    rl, ul, vl, wl, pl_ = left
    rr, ur, vr, wr, pr = right
    al = GAMMA * rl
    ar = GAMMA * rr
    cl = root(al * pl_)
    cr = root(ar * pr)
    jump = ul - ur
    floor = STAR_FLOOR * jnp.minimum(pl_, pr)
    sl = SHOCK * al
    sr = SHOCK * ar
    bl = (1.0 - SHOCK) * al * pl_
    br = (1.0 - SHOCK) * ar * pr

    def star(a, b):
        return jnp.maximum((b * (pl_ + a * jump) + a * pr) * inverse(a + b), floor)

    p = star(cl, cr)
    for _ in range(RIEMANN_ITERS):
        p = star(root(bl + sl * p), root(br + sr * p))
    a = root(bl + sl * p)
    b = root(br + sr * p)
    u = (a * ul + b * ur + (pl_ - pr)) * inverse(a + b)
    up = u > 0.0
    r = jnp.where(up, rl, rr)
    v = jnp.where(up, vl, vr)
    w = jnp.where(up, wl, wr)
    pu = jnp.where(up, pl_, pr)
    m = r * u
    energy = (1.0 / GM1) * pu + 0.5 * r * (u * u + v * v + w * w)
    return m, m * u + p, m * v, m * w, u * (energy + p)


def primitives(state, normal):
    rho = state[0]
    inv = inverse(rho)
    mom = [state[c] for c in normal]
    vel = [m * inv for m in mom]
    kinetic = 0.5 * (mom[0] * vel[0] + mom[1] * vel[1] + mom[2] * vel[2])
    pressure = jnp.maximum(GM1 * (state[4] - kinetic), PRESSURE_FLOOR)
    return [rho] + vel + [pressure]


def line_change(prims, cells):
    left, right = [], []
    for q in prims:
        n = q.shape[0]
        face = face_values(q[0 : n - 3], q[1 : n - 2], q[2 : n - 1], q[3:n])
        lo, hi = cell_edges(q[2 : n - 2], face[: n - 4], face[1:])
        left.append(hi[: cells + 1])
        right.append(lo[1:])
    flux = riemann(left, right)
    return [DTDX * (f[1:] - f[:-1]) for f in flux]


def x_line(load, store):
    lane = lax.broadcasted_iota(jnp.int32, (NZ, 128), 1)

    def shift(tiles, k):
        turned = [pltpu.roll(q, (-k) % 128, axis=1) for q in tiles]
        if k > 0:
            return [jnp.where(lane < 128 - k, turned[t], turned[(t + 1) % TILES]) for t in range(TILES)]
        return [jnp.where(lane >= -k, turned[t], turned[t - 1]) for t in range(TILES)]

    prims = [load(t) for t in range(TILES)]
    left, right = [], []
    for c in range(5):
        q = [prims[t][c] for t in range(TILES)]
        far = [shift(q, -1), q, shift(q, 1), shift(q, 2)]
        face = [face_values(*(f[t] for f in far)) for t in range(TILES)]
        back = shift(face, -1)
        pairs = [cell_edges(q[t], back[t], face[t]) for t in range(TILES)]
        left.append([p[1] for p in pairs])
        right.append(shift([p[0] for p in pairs], 1))
    flux = [riemann([l[t] for l in left], [r[t] for r in right]) for t in range(TILES)]
    before = [shift([f[c] for f in flux], -1) for c in range(5)]
    for t in range(TILES):
        rho, u, v, w, p = load(t)
        kinetic = 0.5 * rho * (u * u + v * v + w * w)
        state = (rho, rho * u, rho * v, rho * w, (1.0 / GM1) * p + kinetic)
        store(t, [state[c] - DTDX * (flux[t][c] - before[c][t]) for c in range(5)])


def x_kernel(d_ref, v_ref, p_ref, s_ref, f_ref, b_ref):
    def line(y, carry):
        def load(t):
            at = pl.ds(t * NY + y, NZ, stride=TILES * NY)
            return d_ref[at, :], v_ref[0, at, :], v_ref[1, at, :], v_ref[2, at, :], p_ref[at, :]

        def store(t, new):
            for c in range(5):
                s_ref[c, y, t] = new[c]

        x_line(load, store)
        return carry

    lax.fori_loop(0, NY, line, 0)
    odd = lax.rem(lax.axis_index("row"), 2)
    f_ref[...] = s_ref[:, pl.ds(odd, HALO)]
    b_ref[...] = s_ref[:, pl.ds(1 - odd, HALO)]


def y_kernel(per, s_ref, f_in, b_in, t_ref, f_ref, b_ref):
    odd = lax.rem(lax.axis_index("row"), 2) == 1
    for t in range(per):
        full = [
            jnp.concatenate(
                [
                    jnp.where(odd, b_in[c, :, t], f_in[c, :, t]),
                    s_ref[c, :, t],
                    jnp.where(odd, f_in[c, :, t], b_in[c, :, t]),
                ],
                axis=0,
            )
            for c in range(5)
        ]
        change = line_change(primitives(full, (2, 1, 3)), NY)
        for c, k in enumerate((0, 2, 1, 3, 4)):
            new = full[c][HALO : HALO + NY] - change[k]
            for y in range(NY):
                t_ref[c, pl.ds(t * NY + y, NZ, stride=per * NY), :] = new[y]
    width = per * NY
    odd = lax.rem(lax.axis_index("col"), 2)
    for c in range(5):
        f_ref[c] = t_ref[c, pl.ds(pl.multiple_of(odd * (NZ - HALO) * width, 8), HALO * width)]
        b_ref[c] = t_ref[c, pl.ds(pl.multiple_of((1 - odd) * (NZ - HALO) * width, 8), HALO * width)]


def z_kernel(per, t_ref, f_in, b_in, o_ref):
    width = per * NY
    odd = lax.rem(lax.axis_index("col"), 2) == 1

    def halo(even_ref, odd_ref, c, z, r):
        at = slice(z * width + r, z * width + r + 8)
        return jnp.where(odd, odd_ref[c, at], even_ref[c, at])

    for r in range(0, width, 8):
        full = [
            jnp.stack(
                [halo(f_in, b_in, c, z, r) for z in range(HALO)]
                + [t_ref[c, z * width + r : z * width + r + 8] for z in range(NZ)]
                + [halo(b_in, f_in, c, z, r) for z in range(HALO)]
            )
            for c in range(5)
        ]
        change = line_change(primitives(full, (3, 1, 2)), NZ)
        for c, k in enumerate((0, 2, 3, 1, 4)):
            new = full[c][HALO : HALO + NZ] - change[k]
            for z in range(NZ):
                o_ref[c, z, r : r + 8] = new[z]


def rows(a):
    lead = a.shape[:-3]
    a = jnp.swapaxes(a.reshape(*lead, NZ, NY, TILES, 128), -2, -3)
    return a.reshape(*lead, NZ * TILES * NY, 128)


def unrows(a):
    a = jnp.swapaxes(a.reshape(5, NZ, TILES, NY, 128), -2, -3)
    return a.reshape(5, NZ, NY, NX)


def shape(*s):
    return jax.ShapeDtypeStruct(s, F32)


SMALL = pltpu.CompilerParams(vmem_limit_bytes=12 << 20)


def local(density, velocity, pressure):
    per = TILES
    width = per * NY
    n = lax.axis_size("row")
    inside = [(i, i ^ 1) for i in range(n)]
    across = [(i, (i + 1 if i % 2 else i - 1) % n) for i in range(n)]
    s, f, b = pl.pallas_call(
        x_kernel,
        out_shape=(shape(5, NY, per, NZ, 128), shape(5, HALO, per, NZ, 128), shape(5, HALO, per, NZ, 128)),
    )(rows(density), rows(velocity), rows(pressure))
    f = lax.ppermute(f, "row", across)
    b = lax.ppermute(b, "row", inside)
    t, f, b = pl.pallas_call(
        lambda *refs: y_kernel(per, *refs),
        out_shape=(shape(5, NZ * width, 128), shape(5, HALO * width, 128), shape(5, HALO * width, 128)),
        compiler_params=SMALL,
    )(s, f, b)
    f = lax.ppermute(f, "col", across)
    b = lax.ppermute(b, "col", inside)
    out = pl.pallas_call(
        lambda *refs: z_kernel(per, *refs), out_shape=shape(5, NZ, width, 128), compiler_params=SMALL
    )(t, f, b)
    return unrows(out)


def solution(mesh):
    placed = (P("col", "row", None), P(None, "col", "row", None), P("col", "row", None))
    return jax.shard_map(
        local, mesh=mesh, in_specs=placed, out_specs=P(None, "col", "row", None), check_vma=False
    )
```

```python
import functools

import jax
import jax.numpy as jnp
from jax import lax
from jax.experimental import pallas as pl
from jax.experimental.pallas import tpu as pltpu
from jax.sharding import PartitionSpec as P

RIEMANN_ITERS = 3
GAMMA = 1.4
GM1 = 0.4
SHOCK = (GAMMA + 1.0) / (2.0 * GAMMA)
DTDX = 0.03
PRESSURE_FLOOR = 0.05
STAR_FLOOR = 0.1

NX, NY, NZ = 1024, 4, 8
TILES = NX // 128
HALO = 3
F32 = jnp.float32


def face_values(q0, q1, q2, q3):
    face = 7.0 / 12.0 * (q1 + q2) - 1.0 / 12.0 * (q0 + q3)
    return jnp.minimum(jnp.maximum(face, jnp.minimum(q1, q2)), jnp.maximum(q1, q2))


def cell_edges(q, face_left, face_right):
    dr = face_right - q
    dl = face_left - q
    br = 2.0 * jnp.abs(dr)
    bl = 2.0 * jnp.abs(dl)
    right = q + jnp.minimum(jnp.maximum(dr, -bl), bl)
    left = q + jnp.minimum(jnp.maximum(dl, -br), br)
    return left, right


def root(x):
    return x * lax.rsqrt(x)


def inverse(x):
    return 1.0 / x


def riemann(left, right):
    rl, ul, vl, wl, pl_ = left
    rr, ur, vr, wr, pr = right
    al = GAMMA * rl
    ar = GAMMA * rr
    cl = root(al * pl_)
    cr = root(ar * pr)
    jump = ul - ur
    floor = STAR_FLOOR * jnp.minimum(pl_, pr)
    sl = SHOCK * al
    sr = SHOCK * ar
    bl = (1.0 - SHOCK) * al * pl_
    br = (1.0 - SHOCK) * ar * pr

    def star(a, b):
        return jnp.maximum((b * (pl_ + a * jump) + a * pr) * inverse(a + b), floor)

    p = star(cl, cr)
    for _ in range(RIEMANN_ITERS):
        p = star(root(bl + sl * p), root(br + sr * p))
    a = root(bl + sl * p)
    b = root(br + sr * p)
    u = (a * ul + b * ur + (pl_ - pr)) * inverse(a + b)
    up = u > 0.0
    r = jnp.where(up, rl, rr)
    v = jnp.where(up, vl, vr)
    w = jnp.where(up, wl, wr)
    pu = jnp.where(up, pl_, pr)
    m = r * u
    energy = (1.0 / GM1) * pu + 0.5 * r * (u * u + v * v + w * w)
    return m, m * u + p, m * v, m * w, u * (energy + p)


def primitives(state, normal):
    rho = state[0]
    inv = inverse(rho)
    mom = [state[c] for c in normal]
    vel = [m * inv for m in mom]
    kinetic = 0.5 * (mom[0] * vel[0] + mom[1] * vel[1] + mom[2] * vel[2])
    pressure = jnp.maximum(GM1 * (state[4] - kinetic), PRESSURE_FLOOR)
    return [rho] + vel + [pressure]


def line_change(prims, cells):
    left, right = [], []
    for q in prims:
        n = q.shape[0]
        face = face_values(q[0 : n - 3], q[1 : n - 2], q[2 : n - 1], q[3:n])
        lo, hi = cell_edges(q[2 : n - 2], face[: n - 4], face[1:])
        left.append(hi[: cells + 1])
        right.append(lo[1:])
    flux = riemann(left, right)
    return [DTDX * (f[1:] - f[:-1]) for f in flux]


def x_line(load, store, m):
    lane = lax.broadcasted_iota(jnp.int32, (NZ, 128), 1)
    last = m + 1

    def shift(tiles, k):
        turned = [pltpu.roll(q, (-k) % 128, axis=1) for q in tiles]
        if k > 0:
            return [jnp.where(lane < 128 - k, turned[t], turned[min(t + 1, last)]) for t in range(m + 2)]
        return [jnp.where(lane >= -k, turned[t], turned[max(t - 1, 0)]) for t in range(m + 2)]

    prims = [load(t) for t in range(-1, m + 1)]
    left, right = [], []
    for c in range(5):
        q = [p[c] for p in prims]
        far = [shift(q, -1), q, shift(q, 1), shift(q, 2)]
        face = [face_values(*(f[t] for f in far)) for t in range(m + 2)]
        back = shift(face, -1)
        pairs = [cell_edges(q[t], back[t], face[t]) for t in range(m + 2)]
        left.append([p[1] for p in pairs])
        right.append(shift([p[0] for p in pairs], 1))
    flux = [riemann([l[t] for l in left], [r[t] for r in right]) for t in range(m + 1)]
    for t in range(m):
        rho, u, v, w, p = load(t)
        kinetic = 0.5 * rho * (u * u + v * v + w * w)
        state = (rho, rho * u, rho * v, rho * w, (1.0 / GM1) * p + kinetic)
        now, old = flux[t + 1], flux[t]
        new = []
        for c in range(5):
            before = jnp.where(lane >= 1, pltpu.roll(now[c], 1, axis=1), pltpu.roll(old[c], 1, axis=1))
            new.append(state[c] - DTDX * (now[c] - before))
        store(t, new)


def x_kernel(start, m, q_ref, s_ref, f_ref, b_ref):
    def line(y, carry):
        def load(t):
            tile = (start + t) % TILES
            return [q_ref[c, pl.ds(tile * NY + y, NZ, stride=TILES * NY), :] for c in range(5)]

        def store(t, new):
            for c in range(5):
                s_ref[c, y, t] = new[c]

        x_line(load, store, m)
        return carry

    lax.fori_loop(0, NY, line, 0)
    odd = lax.rem(lax.axis_index("row"), 2)
    f_ref[...] = s_ref[:, pl.ds(odd, HALO)]
    b_ref[...] = s_ref[:, pl.ds(1 - odd, HALO)]


def y_kernel(per, s_ref, f_in, b_in, t_ref, f_ref, b_ref):
    odd = lax.rem(lax.axis_index("row"), 2) == 1
    for t in range(per):
        full = [
            jnp.concatenate(
                [
                    jnp.where(odd, b_in[c, :, t], f_in[c, :, t]),
                    s_ref[c, :, t],
                    jnp.where(odd, f_in[c, :, t], b_in[c, :, t]),
                ],
                axis=0,
            )
            for c in range(5)
        ]
        change = line_change(primitives(full, (2, 1, 3)), NY)
        for c, k in enumerate((0, 2, 1, 3, 4)):
            new = full[c][HALO : HALO + NY] - change[k]
            for y in range(NY):
                t_ref[c, pl.ds(t * NY + y, NZ, stride=per * NY), :] = new[y]
    width = per * NY
    odd = lax.rem(lax.axis_index("col"), 2)
    for c in range(5):
        f_ref[c] = t_ref[c, pl.ds(pl.multiple_of(odd * (NZ - HALO) * width, 8), HALO * width)]
        b_ref[c] = t_ref[c, pl.ds(pl.multiple_of((1 - odd) * (NZ - HALO) * width, 8), HALO * width)]


def z_kernel(start, per, t_ref, f_in, b_in, _, o_hbm, o_ref, sems):
    width = per * NY
    odd = lax.rem(lax.axis_index("col"), 2) == 1

    def halo(even_ref, odd_ref, c, z, r):
        at = slice(z * width + r, z * width + r + 8)
        return jnp.where(odd, odd_ref[c, at], even_ref[c, at])

    copies = []
    for i, r in enumerate(range(0, width, 8)):
        full = [
            jnp.stack(
                [halo(f_in, b_in, c, z, r) for z in range(HALO)]
                + [t_ref[c, z * width + r : z * width + r + 8] for z in range(NZ)]
                + [halo(b_in, f_in, c, z, r) for z in range(HALO)]
            )
            for c in range(5)
        ]
        change = line_change(primitives(full, (3, 1, 2)), NZ)
        for c, k in enumerate((0, 2, 3, 1, 4)):
            new = full[c][HALO : HALO + NZ] - change[k]
            for z in range(NZ):
                o_ref[c, z, r : r + 8] = new[z]
        copies.append(
            pltpu.make_async_copy(
                o_ref.at[:, :, r : r + 8], o_hbm.at[:, :, start * NY + r : start * NY + r + 8], sems.at[i]
            )
        )
        copies[-1].start()
    for copy in copies:
        copy.wait()


def rows(a):
    lead = a.shape[:-3]
    a = jnp.swapaxes(a.reshape(*lead, NZ, NY, TILES, 128), -2, -3)
    return a.reshape(*lead, NZ * TILES * NY, 128)


def unrows(a):
    a = jnp.swapaxes(a.reshape(5, NZ, TILES, NY, 128), -2, -3)
    return a.reshape(5, NZ, NY, NX)


def cost(m, ops):
    cells = NZ * NY * 128 * m
    return pl.CostEstimate(flops=ops * cells, bytes_accessed=80 * cells, transcendentals=12 * cells)


def shape(*s):
    return jax.ShapeDtypeStruct(s, F32)


SMALL = pltpu.CompilerParams(vmem_limit_bytes=12 << 20)


CUTS = (0, 4, 8)


def local(density, velocity, pressure):
    n = lax.axis_size("row")
    inside = [(i, i ^ 1) for i in range(n)]
    across = [(i, (i + 1 if i % 2 else i - 1) % n) for i in range(n)]
    chunks = [(a, b - a) for a, b in zip(CUTS, CUTS[1:])]
    prims = jnp.concatenate([rows(density)[None], rows(velocity), rows(pressure)[None]])

    def x_sweep(start, m):
        return pl.pallas_call(
            functools.partial(x_kernel, start, m),
            out_shape=(shape(5, NY, m, NZ, 128), shape(5, HALO, m, NZ, 128), shape(5, HALO, m, NZ, 128)),
            compiler_params=SMALL,
            cost_estimate=cost(m, 1500),
            name=f"x{start}",
        )(prims)

    def y_sweep(start, m, s, f, b):
        w = m * NY
        return pl.pallas_call(
            functools.partial(y_kernel, m),
            out_shape=(shape(5, NZ * w, 128), shape(5, HALO * w, 128), shape(5, HALO * w, 128)),
            compiler_params=SMALL,
            cost_estimate=cost(m, 1000),
            name=f"y{start}",
        )(s, f, b)

    def z_sweep(start, m, t, f, b, out):
        w = m * NY
        first = out is None
        near = pl.BlockSpec(memory_space=pltpu.VMEM)
        far = pl.BlockSpec(memory_space=pl.ANY)
        kernel = functools.partial(z_kernel, start, m)
        return pl.pallas_call(
            (lambda t, f, b, *rest: kernel(t, f, b, None, *rest)) if first else kernel,
            in_specs=[near] * 3 + [far] * (not first),
            out_specs=far,
            out_shape=shape(5, NZ, TILES * NY, 128),
            scratch_shapes=[pltpu.VMEM((5, NZ, w, 128), F32), pltpu.SemaphoreType.DMA((w // 8,))],
            input_output_aliases={} if first else {3: 0},
            compiler_params=SMALL,
            cost_estimate=cost(m, 1000),
            name=f"z{start}",
        )(t, f, b, *([] if first else [out]))

    y_in = []
    for start, m in chunks:
        s, f, b = x_sweep(start, m)
        y_in.append((s, lax.ppermute(f, "row", across), lax.ppermute(b, "row", inside)))
    z_in = []
    for (start, m), args in zip(chunks, y_in):
        t, f, b = y_sweep(start, m, *args)
        z_in.append((t, lax.ppermute(b, "col", inside), lax.ppermute(f, "col", across)))
    out = None
    for (start, m), (t, b, f) in zip(chunks, z_in):
        out = z_sweep(start, m, t, f, b, out)
    return unrows(out)


def solution(mesh):
    placed = (P("col", "row", None), P(None, "col", "row", None), P("col", "row", None))
    return jax.shard_map(
        local, mesh=mesh, in_specs=placed, out_specs=P(None, "col", "row", None), check_vma=False
    )
```

```python
import functools

import jax
import jax.numpy as jnp
from jax import lax
from jax.experimental import pallas as pl
from jax.experimental.pallas import tpu as pltpu
from jax.sharding import PartitionSpec as P

RIEMANN_ITERS = 3
GAMMA = 1.4
GM1 = 0.4
SHOCK = (GAMMA + 1.0) / (2.0 * GAMMA)
DTDX = 0.03
PRESSURE_FLOOR = 0.05
STAR_FLOOR = 0.1

NX, NY, NZ = 1024, 4, 8
TILES = NX // 128
HALO = 3
F32 = jnp.float32


def face_values(q0, q1, q2, q3):
    face = 7.0 / 12.0 * (q1 + q2) - 1.0 / 12.0 * (q0 + q3)
    return jnp.minimum(jnp.maximum(face, jnp.minimum(q1, q2)), jnp.maximum(q1, q2))


def cell_edges(q, face_left, face_right):
    dr = face_right - q
    dl = face_left - q
    br = 2.0 * jnp.abs(dr)
    bl = 2.0 * jnp.abs(dl)
    right = q + jnp.minimum(jnp.maximum(dr, -bl), bl)
    left = q + jnp.minimum(jnp.maximum(dl, -br), br)
    return left, right


def root(x):
    return x * lax.rsqrt(x)


def inverse(x):
    return 1.0 / x


def riemann(left, right):
    rl, ul, vl, wl, pl_ = left
    rr, ur, vr, wr, pr = right
    al = GAMMA * rl
    ar = GAMMA * rr
    cl = root(al * pl_)
    cr = root(ar * pr)
    jump = ul - ur
    floor = STAR_FLOOR * jnp.minimum(pl_, pr)
    sl = SHOCK * al
    sr = SHOCK * ar
    bl = (1.0 - SHOCK) * al * pl_
    br = (1.0 - SHOCK) * ar * pr

    def star(a, b):
        return jnp.maximum((b * (pl_ + a * jump) + a * pr) * inverse(a + b), floor)

    p = star(cl, cr)
    for _ in range(RIEMANN_ITERS):
        p = star(root(bl + sl * p), root(br + sr * p))
    a = root(bl + sl * p)
    b = root(br + sr * p)
    u = (a * ul + b * ur + (pl_ - pr)) * inverse(a + b)
    up = u > 0.0
    r = jnp.where(up, rl, rr)
    v = jnp.where(up, vl, vr)
    w = jnp.where(up, wl, wr)
    pu = jnp.where(up, pl_, pr)
    m = r * u
    energy = (1.0 / GM1) * pu + 0.5 * r * (u * u + v * v + w * w)
    return m, m * u + p, m * v, m * w, u * (energy + p)


def primitives(state, normal):
    rho = state[0]
    inv = inverse(rho)
    mom = [state[c] for c in normal]
    vel = [m * inv for m in mom]
    kinetic = 0.5 * (mom[0] * vel[0] + mom[1] * vel[1] + mom[2] * vel[2])
    pressure = jnp.maximum(GM1 * (state[4] - kinetic), PRESSURE_FLOOR)
    return [rho] + vel + [pressure]


def line_change(prims, cells):
    left, right = [], []
    for q in prims:
        n = q.shape[0]
        face = face_values(q[0 : n - 3], q[1 : n - 2], q[2 : n - 1], q[3:n])
        lo, hi = cell_edges(q[2 : n - 2], face[: n - 4], face[1:])
        left.append(hi[: cells + 1])
        right.append(lo[1:])
    flux = riemann(left, right)
    return [DTDX * (f[1:] - f[:-1]) for f in flux]


def x_line(tiles, store, m):
    lane = lax.broadcasted_iota(jnp.int32, (NZ, 128), 1)
    ring = len(tiles)

    def shift(row, k):
        turned = [pltpu.roll(q, (-k) % 128, axis=1) for q in row]
        if k > 0:
            return [jnp.where(lane < 128 - k, turned[t], turned[(t + 1) % ring]) for t in range(ring)]
        return [jnp.where(lane >= -k, turned[t], turned[t - 1]) for t in range(ring)]

    left, right = [], []
    for c in range(5):
        q = [p[c] for p in tiles]
        far = [shift(q, -1), q, shift(q, 1), shift(q, 2)]
        face = [face_values(*(f[t] for f in far)) for t in range(ring)]
        back = shift(face, -1)
        pairs = [cell_edges(q[t], back[t], face[t]) for t in range(ring)]
        left.append([p[1] for p in pairs])
        right.append(shift([p[0] for p in pairs], 1))
    flux = [riemann([l[t] for l in left], [r[t] for r in right]) for t in range(ring)]
    turned = [[pltpu.roll(f, 1, axis=1) for f in fs] for fs in flux]
    for t in range(m):
        rho, u, v, w, p = tiles[t]
        kinetic = 0.5 * rho * (u * u + v * v + w * w)
        state = (rho, rho * u, rho * v, rho * w, (1.0 / GM1) * p + kinetic)
        new = []
        for c in range(5):
            before = jnp.where(lane >= 1, turned[t][c], turned[t - 1][c])
            new.append(state[c] - DTDX * (flux[t][c] - before))
        store(t, new)


def x_kernel(start, m, q_ref, s_ref, f_ref, b_ref):
    lane = lax.broadcasted_iota(jnp.int32, (NZ, 128), 1)

    def line(y, carry):
        def load(t):
            tile = (start + t) % TILES
            return [q_ref[c, pl.ds(tile * NY + y, NZ, stride=TILES * NY), :] for c in range(5)]

        def store(t, new):
            for c in range(5):
                s_ref[c, y, t] = new[c]

        tiles = [load(t) for t in range(m)]
        if m < TILES:
            tiles.append([jnp.where(lane < 64, hi, lo) for hi, lo in zip(load(m), load(-1))])
        x_line(tiles, store, m)
        return carry

    lax.fori_loop(0, NY, line, 0)
    odd = lax.rem(lax.axis_index("row"), 2)
    f_ref[...] = s_ref[:, pl.ds(odd, HALO)]
    b_ref[...] = s_ref[:, pl.ds(1 - odd, HALO)]


def y_kernel(per, s_ref, f_in, b_in, t_ref, f_ref, b_ref):
    odd = lax.rem(lax.axis_index("row"), 2) == 1
    for t in range(per):
        full = [
            jnp.concatenate(
                [
                    jnp.where(odd, b_in[c, :, t], f_in[c, :, t]),
                    s_ref[c, :, t],
                    jnp.where(odd, f_in[c, :, t], b_in[c, :, t]),
                ],
                axis=0,
            )
            for c in range(5)
        ]
        change = line_change(primitives(full, (2, 1, 3)), NY)
        for c, k in enumerate((0, 2, 1, 3, 4)):
            new = full[c][HALO : HALO + NY] - change[k]
            for y in range(NY):
                t_ref[c, pl.ds(t * NY + y, NZ, stride=per * NY), :] = new[y]
    width = per * NY
    odd = lax.rem(lax.axis_index("col"), 2)
    for c in range(5):
        f_ref[c] = t_ref[c, pl.ds(pl.multiple_of(odd * (NZ - HALO) * width, 8), HALO * width)]
        b_ref[c] = t_ref[c, pl.ds(pl.multiple_of((1 - odd) * (NZ - HALO) * width, 8), HALO * width)]


def z_kernel(start, per, t_ref, b_in, f_in, _, o_hbm, o_ref, sems):
    width = per * NY
    odd = lax.rem(lax.axis_index("col"), 2) == 1

    def halo(even_ref, odd_ref, c, z, r):
        at = slice(z * width + r, z * width + r + 8)
        return jnp.where(odd, odd_ref[c, at], even_ref[c, at])

    copies = []
    for i, r in enumerate(range(0, width, 8)):
        full = [
            jnp.stack(
                [halo(f_in, b_in, c, z, r) for z in range(HALO)]
                + [t_ref[c, z * width + r : z * width + r + 8] for z in range(NZ)]
                + [halo(b_in, f_in, c, z, r) for z in range(HALO)]
            )
            for c in range(5)
        ]
        change = line_change(primitives(full, (3, 1, 2)), NZ)
        for c, k in enumerate((0, 2, 3, 1, 4)):
            new = full[c][HALO : HALO + NZ] - change[k]
            for z in range(NZ):
                o_ref[c, z, r : r + 8] = new[z]
        copies.append(
            pltpu.make_async_copy(
                o_ref.at[:, :, r : r + 8], o_hbm.at[:, :, start * NY + r : start * NY + r + 8], sems.at[i]
            )
        )
        copies[-1].start()
    for copy in copies:
        copy.wait()


def rows(a):
    lead = a.shape[:-3]
    a = jnp.swapaxes(a.reshape(*lead, NZ, NY, TILES, 128), -2, -3)
    return a.reshape(*lead, NZ * TILES * NY, 128)


def unrows(a):
    a = jnp.swapaxes(a.reshape(5, NZ, TILES, NY, 128), -2, -3)
    return a.reshape(5, NZ, NY, NX)


def cost(m, ops):
    cells = NZ * NY * 128 * m
    return pl.CostEstimate(flops=ops * cells, bytes_accessed=80 * cells, transcendentals=12 * cells)


def shape(*s):
    return jax.ShapeDtypeStruct(s, F32)


SMALL = pltpu.CompilerParams(vmem_limit_bytes=12 << 20)


CUTS = (0, 4, 8)


def local(density, velocity, pressure):
    n = lax.axis_size("row")
    inside = [(i, i ^ 1) for i in range(n)]
    across = [(i, (i + 1 if i % 2 else i - 1) % n) for i in range(n)]
    chunks = [(a, b - a) for a, b in zip(CUTS, CUTS[1:])]
    prims = jnp.concatenate([rows(density)[None], rows(velocity), rows(pressure)[None]])

    def x_sweep(start, m):
        return pl.pallas_call(
            functools.partial(x_kernel, start, m),
            out_shape=(shape(5, NY, m, NZ, 128), shape(5, HALO, m, NZ, 128), shape(5, HALO, m, NZ, 128)),
            compiler_params=SMALL,
            cost_estimate=cost(m, 1500),
            name=f"x{start}",
        )(prims)

    def y_sweep(start, m, s, f, b):
        w = m * NY
        return pl.pallas_call(
            functools.partial(y_kernel, m),
            out_shape=(shape(5, NZ * w, 128), shape(5, HALO * w, 128), shape(5, HALO * w, 128)),
            compiler_params=SMALL,
            cost_estimate=cost(m, 1000),
            name=f"y{start}",
        )(s, f, b)

    def z_sweep(start, m, t, f, b, out):
        w = m * NY
        first = out is None
        near = pl.BlockSpec(memory_space=pltpu.VMEM)
        far = pl.BlockSpec(memory_space=pl.ANY)
        kernel = functools.partial(z_kernel, start, m)
        return pl.pallas_call(
            (lambda t, b, f, *rest: kernel(t, b, f, None, *rest)) if first else kernel,
            in_specs=[near] * 3 + [far] * (not first),
            out_specs=far,
            out_shape=shape(5, NZ, TILES * NY, 128),
            scratch_shapes=[pltpu.VMEM((5, NZ, w, 128), F32), pltpu.SemaphoreType.DMA((w // 8,))],
            input_output_aliases={} if first else {3: 0},
            compiler_params=SMALL,
            cost_estimate=cost(m, 1000),
            name=f"z{start}",
        )(t, b, f, *([] if first else [out]))

    y_in = []
    for start, m in chunks:
        s, f, b = x_sweep(start, m)
        y_in.append((s, lax.ppermute(f, "row", across), lax.ppermute(b, "row", inside)))
    z_in = []
    for (start, m), args in zip(chunks, y_in):
        t, f, b = y_sweep(start, m, *args)
        z_in.append((t, lax.ppermute(b, "col", inside), lax.ppermute(f, "col", across)))
    out = None
    for (start, m), (t, b, f) in zip(chunks, z_in):
        out = z_sweep(start, m, t, f, b, out)
    return unrows(out)


def solution(mesh):
    placed = (P("col", "row", None), P(None, "col", "row", None), P("col", "row", None))
    return jax.shard_map(
        local, mesh=mesh, in_specs=placed, out_specs=P(None, "col", "row", None), check_vma=False
    )
```

```python
import functools

import jax
import jax.numpy as jnp
from jax import lax
from jax.experimental import pallas as pl
from jax.experimental.pallas import tpu as pltpu
from jax.sharding import PartitionSpec as P

RIEMANN_ITERS = 3
GAMMA = 1.4
GM1 = 0.4
SHOCK = (GAMMA + 1.0) / (2.0 * GAMMA)
DTDX = 0.03
PRESSURE_FLOOR = 0.05
STAR_FLOOR = 0.1

NX, NY, NZ = 1024, 4, 8
TILES = NX // 128
HALO = 3
F32 = jnp.float32


def face_values(q0, q1, q2, q3):
    face = 7.0 / 12.0 * (q1 + q2) - 1.0 / 12.0 * (q0 + q3)
    return jnp.minimum(jnp.maximum(face, jnp.minimum(q1, q2)), jnp.maximum(q1, q2))


def cell_edges(q, face_left, face_right):
    dr = face_right - q
    dl = face_left - q
    br = 2.0 * jnp.abs(dr)
    bl = 2.0 * jnp.abs(dl)
    right = q + jnp.minimum(jnp.maximum(dr, -bl), bl)
    left = q + jnp.minimum(jnp.maximum(dl, -br), br)
    return left, right


def root(x):
    return x * lax.rsqrt(x)


def inverse(x):
    return 1.0 / x


def riemann(left, right):
    rl, ul, vl, wl, pl_ = left
    rr, ur, vr, wr, pr = right
    al = GAMMA * rl
    ar = GAMMA * rr
    cl = root(al * pl_)
    cr = root(ar * pr)
    jump = ul - ur
    floor = STAR_FLOOR * jnp.minimum(pl_, pr)
    sl = SHOCK * al
    sr = SHOCK * ar
    bl = (1.0 - SHOCK) * al * pl_
    br = (1.0 - SHOCK) * ar * pr

    def star(a, b):
        return jnp.maximum((b * (pl_ + a * jump) + a * pr) * inverse(a + b), floor)

    p = star(cl, cr)
    for _ in range(RIEMANN_ITERS):
        p = star(root(bl + sl * p), root(br + sr * p))
    a = root(bl + sl * p)
    b = root(br + sr * p)
    u = (a * ul + b * ur + (pl_ - pr)) * inverse(a + b)
    up = u > 0.0
    r = jnp.where(up, rl, rr)
    v = jnp.where(up, vl, vr)
    w = jnp.where(up, wl, wr)
    pu = jnp.where(up, pl_, pr)
    m = r * u
    energy = (1.0 / GM1) * pu + 0.5 * r * (u * u + v * v + w * w)
    return m, m * u + p, m * v, m * w, u * (energy + p)


def primitives(state, normal):
    rho = state[0]
    inv = inverse(rho)
    mom = [state[c] for c in normal]
    vel = [m * inv for m in mom]
    kinetic = 0.5 * (mom[0] * vel[0] + mom[1] * vel[1] + mom[2] * vel[2])
    pressure = jnp.maximum(GM1 * (state[4] - kinetic), PRESSURE_FLOOR)
    return [rho] + vel + [pressure]


def line_change(prims, cells):
    left, right = [], []
    for q in prims:
        n = q.shape[0]
        face = face_values(q[0 : n - 3], q[1 : n - 2], q[2 : n - 1], q[3:n])
        lo, hi = cell_edges(q[2 : n - 2], face[: n - 4], face[1:])
        left.append(hi[: cells + 1])
        right.append(lo[1:])
    flux = riemann(left, right)
    return [DTDX * (f[1:] - f[:-1]) for f in flux]


def x_line(tiles, store, m):
    lane = lax.broadcasted_iota(jnp.int32, (NZ, 128), 1)
    ring = len(tiles)

    def shift(row, k):
        turned = [pltpu.roll(q, (-k) % 128, axis=1) for q in row]
        if k > 0:
            return [jnp.where(lane < 128 - k, turned[t], turned[(t + 1) % ring]) for t in range(ring)]
        return [jnp.where(lane >= -k, turned[t], turned[t - 1]) for t in range(ring)]

    left, right = [], []
    for c in range(5):
        q = [p[c] for p in tiles]
        far = [shift(q, -1), q, shift(q, 1), shift(q, 2)]
        face = [face_values(*(f[t] for f in far)) for t in range(ring)]
        back = shift(face, -1)
        pairs = [cell_edges(q[t], back[t], face[t]) for t in range(ring)]
        left.append([p[1] for p in pairs])
        right.append(shift([p[0] for p in pairs], 1))
    flux = [riemann([l[t] for l in left], [r[t] for r in right]) for t in range(ring)]
    turned = [[pltpu.roll(f, 1, axis=1) for f in fs] for fs in flux]
    for t in range(m):
        rho, u, v, w, p = tiles[t]
        kinetic = 0.5 * rho * (u * u + v * v + w * w)
        state = (rho, rho * u, rho * v, rho * w, (1.0 / GM1) * p + kinetic)
        new = []
        for c in range(5):
            before = jnp.where(lane >= 1, turned[t][c], turned[t - 1][c])
            new.append(state[c] - DTDX * (flux[t][c] - before))
        store(t, new)


def x_kernel(start, m, q_ref, s_ref, f_ref, b_ref):
    lane = lax.broadcasted_iota(jnp.int32, (NZ, 128), 1)

    def line(y, carry):
        def load(t):
            tile = (start + t) % TILES
            return [q_ref[c, pl.ds(tile * NY + y, NZ, stride=TILES * NY), :] for c in range(5)]

        def store(t, new):
            for c in range(5):
                s_ref[c, y, t] = new[c]

        tiles = [load(t) for t in range(m)]
        if m < TILES:
            tiles.append([jnp.where(lane < 64, hi, lo) for hi, lo in zip(load(m), load(-1))])
        x_line(tiles, store, m)
        return carry

    lax.fori_loop(0, NY, line, 0, unroll=2)
    odd = lax.rem(lax.axis_index("row"), 2)
    f_ref[...] = s_ref[:, pl.ds(odd, HALO)]
    b_ref[...] = s_ref[:, pl.ds(1 - odd, HALO)]


def y_kernel(per, s_ref, f_in, b_in, t_ref, f_ref, b_ref):
    odd = lax.rem(lax.axis_index("row"), 2) == 1
    for t in range(per):
        full = [
            jnp.concatenate(
                [
                    jnp.where(odd, b_in[c, :, t], f_in[c, :, t]),
                    s_ref[c, :, t],
                    jnp.where(odd, f_in[c, :, t], b_in[c, :, t]),
                ],
                axis=0,
            )
            for c in range(5)
        ]
        change = line_change(primitives(full, (2, 1, 3)), NY)
        for c, k in enumerate((0, 2, 1, 3, 4)):
            new = full[c][HALO : HALO + NY] - change[k]
            for y in range(NY):
                t_ref[c, pl.ds(t * NY + y, NZ, stride=per * NY), :] = new[y]
    width = per * NY
    odd = lax.rem(lax.axis_index("col"), 2)
    for c in range(5):
        f_ref[c] = t_ref[c, pl.ds(pl.multiple_of(odd * (NZ - HALO) * width, 8), HALO * width)]
        b_ref[c] = t_ref[c, pl.ds(pl.multiple_of((1 - odd) * (NZ - HALO) * width, 8), HALO * width)]


def z_kernel(start, per, t_ref, b_in, f_in, _, o_hbm, o_ref, sems):
    width = per * NY
    odd = lax.rem(lax.axis_index("col"), 2) == 1

    def halo(even_ref, odd_ref, c, z, r):
        at = slice(z * width + r, z * width + r + 8)
        return jnp.where(odd, odd_ref[c, at], even_ref[c, at])

    copies = []
    for i, r in enumerate(range(0, width, 8)):
        full = [
            jnp.stack(
                [halo(f_in, b_in, c, z, r) for z in range(HALO)]
                + [t_ref[c, z * width + r : z * width + r + 8] for z in range(NZ)]
                + [halo(b_in, f_in, c, z, r) for z in range(HALO)]
            )
            for c in range(5)
        ]
        change = line_change(primitives(full, (3, 1, 2)), NZ)
        for c, k in enumerate((0, 2, 3, 1, 4)):
            new = full[c][HALO : HALO + NZ] - change[k]
            for z in range(NZ):
                o_ref[c, z, r : r + 8] = new[z]
        copies.append(
            pltpu.make_async_copy(
                o_ref.at[:, :, r : r + 8], o_hbm.at[:, :, start * NY + r : start * NY + r + 8], sems.at[i]
            )
        )
        copies[-1].start()
    for copy in copies:
        copy.wait()


def rows(a):
    lead = a.shape[:-3]
    a = jnp.swapaxes(a.reshape(*lead, NZ, NY, TILES, 128), -2, -3)
    return a.reshape(*lead, NZ * TILES * NY, 128)


def unrows(a):
    a = jnp.swapaxes(a.reshape(5, NZ, TILES, NY, 128), -2, -3)
    return a.reshape(5, NZ, NY, NX)


def cost(m, ops):
    cells = NZ * NY * 128 * m
    return pl.CostEstimate(flops=ops * cells, bytes_accessed=80 * cells, transcendentals=12 * cells)


def shape(*s):
    return jax.ShapeDtypeStruct(s, F32)


SMALL = pltpu.CompilerParams(vmem_limit_bytes=12 << 20)


CUTS = (0, 4, 8)


def local(density, velocity, pressure):
    n = lax.axis_size("row")
    inside = [(i, i ^ 1) for i in range(n)]
    across = [(i, (i + 1 if i % 2 else i - 1) % n) for i in range(n)]
    chunks = [(a, b - a) for a, b in zip(CUTS, CUTS[1:])]
    prims = jnp.concatenate([rows(density)[None], rows(velocity), rows(pressure)[None]])

    def x_sweep(start, m):
        return pl.pallas_call(
            functools.partial(x_kernel, start, m),
            out_shape=(shape(5, NY, m, NZ, 128), shape(5, HALO, m, NZ, 128), shape(5, HALO, m, NZ, 128)),
            compiler_params=SMALL,
            cost_estimate=cost(m, 1500),
            name=f"x{start}",
        )(prims)

    def y_sweep(start, m, s, f, b):
        w = m * NY
        return pl.pallas_call(
            functools.partial(y_kernel, m),
            out_shape=(shape(5, NZ * w, 128), shape(5, HALO * w, 128), shape(5, HALO * w, 128)),
            compiler_params=SMALL,
            cost_estimate=cost(m, 1000),
            name=f"y{start}",
        )(s, f, b)

    def z_sweep(start, m, t, f, b, out):
        w = m * NY
        first = out is None
        near = pl.BlockSpec(memory_space=pltpu.VMEM)
        far = pl.BlockSpec(memory_space=pl.ANY)
        kernel = functools.partial(z_kernel, start, m)
        return pl.pallas_call(
            (lambda t, b, f, *rest: kernel(t, b, f, None, *rest)) if first else kernel,
            in_specs=[near] * 3 + [far] * (not first),
            out_specs=far,
            out_shape=shape(5, NZ, TILES * NY, 128),
            scratch_shapes=[pltpu.VMEM((5, NZ, w, 128), F32), pltpu.SemaphoreType.DMA((w // 8,))],
            input_output_aliases={} if first else {3: 0},
            compiler_params=SMALL,
            cost_estimate=cost(m, 1000),
            name=f"z{start}",
        )(t, b, f, *([] if first else [out]))

    y_in = []
    for start, m in chunks:
        s, f, b = x_sweep(start, m)
        y_in.append((s, lax.ppermute(f, "row", across), lax.ppermute(b, "row", inside)))
    z_in = []
    for (start, m), args in zip(chunks, y_in):
        t, f, b = y_sweep(start, m, *args)
        z_in.append((t, lax.ppermute(b, "col", inside), lax.ppermute(f, "col", across)))
    out = None
    for (start, m), (t, b, f) in zip(chunks, z_in):
        out = z_sweep(start, m, t, f, b, out)
    return unrows(out)


def solution(mesh):
    placed = (P("col", "row", None), P(None, "col", "row", None), P("col", "row", None))
    return jax.shard_map(
        local, mesh=mesh, in_specs=placed, out_specs=P(None, "col", "row", None), check_vma=False
    )
```

```python
import functools

import jax
import jax.numpy as jnp
from jax import lax
from jax.experimental import pallas as pl
from jax.experimental.pallas import tpu as pltpu
from jax.sharding import PartitionSpec as P

RIEMANN_ITERS = 3
GAMMA = 1.4
GM1 = 0.4
SHOCK = (GAMMA + 1.0) / (2.0 * GAMMA)
DTDX = 0.03
PRESSURE_FLOOR = 0.05
STAR_FLOOR = 0.1

NX, NY, NZ = 1024, 4, 8
TILES = NX // 128
HALO = 3
F32 = jnp.float32


def face_values(q0, q1, q2, q3):
    face = 7.0 / 12.0 * (q1 + q2) - 1.0 / 12.0 * (q0 + q3)
    return jnp.minimum(jnp.maximum(face, jnp.minimum(q1, q2)), jnp.maximum(q1, q2))


def cell_edges(q, face_left, face_right):
    dr = face_right - q
    dl = face_left - q
    br = 2.0 * jnp.abs(dr)
    bl = 2.0 * jnp.abs(dl)
    right = q + jnp.minimum(jnp.maximum(dr, -bl), bl)
    left = q + jnp.minimum(jnp.maximum(dl, -br), br)
    return left, right


def root(x):
    return x * lax.rsqrt(x)


def inverse(x):
    return 1.0 / x


def riemann(left, right):
    rl, ul, vl, wl, pl_ = left
    rr, ur, vr, wr, pr = right
    al = GAMMA * rl
    ar = GAMMA * rr
    cl = root(al * pl_)
    cr = root(ar * pr)
    jump = ul - ur
    floor = STAR_FLOOR * jnp.minimum(pl_, pr)
    sl = SHOCK * al
    sr = SHOCK * ar
    bl = (1.0 - SHOCK) * al * pl_
    br = (1.0 - SHOCK) * ar * pr

    def star(a, b):
        return jnp.maximum((b * (pl_ + a * jump) + a * pr) * inverse(a + b), floor)

    p = star(cl, cr)
    for _ in range(RIEMANN_ITERS):
        p = star(root(bl + sl * p), root(br + sr * p))
    a = root(bl + sl * p)
    b = root(br + sr * p)
    u = (a * ul + b * ur + (pl_ - pr)) * inverse(a + b)
    up = u > 0.0
    r = jnp.where(up, rl, rr)
    v = jnp.where(up, vl, vr)
    w = jnp.where(up, wl, wr)
    pu = jnp.where(up, pl_, pr)
    m = r * u
    energy = (1.0 / GM1) * pu + 0.5 * r * (u * u + v * v + w * w)
    return m, m * u + p, m * v, m * w, u * (energy + p)


def primitives(state, normal):
    rho = state[0]
    inv = inverse(rho)
    mom = [state[c] for c in normal]
    vel = [m * inv for m in mom]
    kinetic = 0.5 * (mom[0] * vel[0] + mom[1] * vel[1] + mom[2] * vel[2])
    pressure = jnp.maximum(GM1 * (state[4] - kinetic), PRESSURE_FLOOR)
    return [rho] + vel + [pressure]


def line_change(prims, cells):
    left, right = [], []
    for q in prims:
        n = q.shape[0]
        face = face_values(q[0 : n - 3], q[1 : n - 2], q[2 : n - 1], q[3:n])
        lo, hi = cell_edges(q[2 : n - 2], face[: n - 4], face[1:])
        left.append(hi[: cells + 1])
        right.append(lo[1:])
    flux = riemann(left, right)
    return [DTDX * (f[1:] - f[:-1]) for f in flux]


def x_kernel(start, m, q_ref, s_ref, f_ref, b_ref, work, done):
    rows_per = NY * NZ
    lanes = m * rows_per
    lane = lax.broadcasted_iota(jnp.int32, (8, lanes), 1)

    def tile(c, t):
        at = (start + t) % TILES * NY
        return [q_ref[c, pl.ds(at + y, NZ, stride=TILES * NY), :] for y in range(NY)]

    for c in range(5):
        own = jnp.concatenate([r for t in range(m) for r in tile(c, t)], axis=0).T
        before, behind = tile(c, -1), tile(c, m)
        edge = jnp.concatenate(before * (m - 1) + behind, axis=0).T
        work[c, 8:136] = own
        work[c, 0:8] = jnp.where(lane < rows_per, edge[120:], pltpu.roll(own[120:], rows_per, axis=1))
        work[c, 136:144] = jnp.where(lane >= lanes - rows_per, edge[:8], pltpu.roll(own[:8], lanes - rows_per, axis=1))
    cells = 16
    prims, faces, edges, flux = [], [], [], None
    for k in range(cells + 2 * HALO):
        prims.append([work[c, pl.ds(8 + k - HALO, 8, stride=cells), :] for c in range(5)])
        if k < 3:
            continue
        faces.append([face_values(*(prims[k - 3 + i][c] for i in range(4))) for c in range(5)])
        if k < 4:
            continue
        edges.append([cell_edges(prims[k - 2][c], faces[-2][c], faces[-1][c]) for c in range(5)])
        if k < 5:
            continue
        now = riemann([e[1] for e in edges[-2]], [e[0] for e in edges[-1]])
        if k > 5:
            rho, u, v, w, p = prims[k - 3]
            kinetic = 0.5 * rho * (u * u + v * v + w * w)
            state = (rho, rho * u, rho * v, rho * w, (1.0 / GM1) * p + kinetic)
            for c in range(5):
                done[c, pl.ds(k - 6, 8, stride=cells), :] = state[c] - DTDX * (now[c] - flux[c])
        flux = now
    for c in range(5):
        back = done[c].T
        for t in range(m):
            for y in range(NY):
                s_ref[c, y, t] = back[(t * NY + y) * NZ : (t * NY + y + 1) * NZ]
    odd = lax.rem(lax.axis_index("row"), 2)
    f_ref[...] = s_ref[:, pl.ds(odd, HALO)]
    b_ref[...] = s_ref[:, pl.ds(1 - odd, HALO)]


def y_kernel(per, s_ref, f_in, b_in, t_ref, f_ref, b_ref):
    odd = lax.rem(lax.axis_index("row"), 2) == 1
    for t in range(per):
        full = [
            jnp.concatenate(
                [
                    jnp.where(odd, b_in[c, :, t], f_in[c, :, t]),
                    s_ref[c, :, t],
                    jnp.where(odd, f_in[c, :, t], b_in[c, :, t]),
                ],
                axis=0,
            )
            for c in range(5)
        ]
        change = line_change(primitives(full, (2, 1, 3)), NY)
        for c, k in enumerate((0, 2, 1, 3, 4)):
            new = full[c][HALO : HALO + NY] - change[k]
            for y in range(NY):
                t_ref[c, pl.ds(t * NY + y, NZ, stride=per * NY), :] = new[y]
    width = per * NY
    odd = lax.rem(lax.axis_index("col"), 2)
    for c in range(5):
        f_ref[c] = t_ref[c, pl.ds(pl.multiple_of(odd * (NZ - HALO) * width, 8), HALO * width)]
        b_ref[c] = t_ref[c, pl.ds(pl.multiple_of((1 - odd) * (NZ - HALO) * width, 8), HALO * width)]


def z_kernel(start, per, t_ref, b_in, f_in, _, o_hbm, o_ref, sems):
    width = per * NY
    odd = lax.rem(lax.axis_index("col"), 2) == 1

    def halo(even_ref, odd_ref, c, z, r):
        at = slice(z * width + r, z * width + r + 8)
        return jnp.where(odd, odd_ref[c, at], even_ref[c, at])

    copies = []
    for i, r in enumerate(range(0, width, 8)):
        full = [
            jnp.stack(
                [halo(f_in, b_in, c, z, r) for z in range(HALO)]
                + [t_ref[c, z * width + r : z * width + r + 8] for z in range(NZ)]
                + [halo(b_in, f_in, c, z, r) for z in range(HALO)]
            )
            for c in range(5)
        ]
        change = line_change(primitives(full, (3, 1, 2)), NZ)
        for c, k in enumerate((0, 2, 3, 1, 4)):
            new = full[c][HALO : HALO + NZ] - change[k]
            for z in range(NZ):
                o_ref[c, z, r : r + 8] = new[z]
        copies.append(
            pltpu.make_async_copy(
                o_ref.at[:, :, r : r + 8], o_hbm.at[:, :, start * NY + r : start * NY + r + 8], sems.at[i]
            )
        )
        copies[-1].start()
    for copy in copies:
        copy.wait()


def rows(a):
    lead = a.shape[:-3]
    a = jnp.swapaxes(a.reshape(*lead, NZ, NY, TILES, 128), -2, -3)
    return a.reshape(*lead, NZ * TILES * NY, 128)


def unrows(a):
    a = jnp.swapaxes(a.reshape(5, NZ, TILES, NY, 128), -2, -3)
    return a.reshape(5, NZ, NY, NX)


def cost(m, ops):
    cells = NZ * NY * 128 * m
    return pl.CostEstimate(flops=ops * cells, bytes_accessed=80 * cells, transcendentals=12 * cells)


def shape(*s):
    return jax.ShapeDtypeStruct(s, F32)


SMALL = pltpu.CompilerParams(vmem_limit_bytes=12 << 20)


CUTS = (0, 4, 8)


def local(density, velocity, pressure):
    n = lax.axis_size("row")
    inside = [(i, i ^ 1) for i in range(n)]
    across = [(i, (i + 1 if i % 2 else i - 1) % n) for i in range(n)]
    chunks = [(a, b - a) for a, b in zip(CUTS, CUTS[1:])]
    prims = jnp.concatenate([rows(density)[None], rows(velocity), rows(pressure)[None]])

    def x_sweep(start, m):
        return pl.pallas_call(
            functools.partial(x_kernel, start, m),
            out_shape=(shape(5, NY, m, NZ, 128), shape(5, HALO, m, NZ, 128), shape(5, HALO, m, NZ, 128)),
            compiler_params=SMALL,
            scratch_shapes=[pltpu.VMEM((5, 144, m * NY * NZ), F32), pltpu.VMEM((5, 128, m * NY * NZ), F32)],
            cost_estimate=cost(m, 1500),
            name=f"x{start}",
        )(prims)

    def y_sweep(start, m, s, f, b):
        w = m * NY
        kernel = functools.partial(y_kernel, m)
        swapped = start > 0
        return pl.pallas_call(
            (lambda s, b, f, *rest: kernel(s, f, b, *rest)) if swapped else kernel,
            out_shape=(shape(5, NZ * w, 128), shape(5, HALO * w, 128), shape(5, HALO * w, 128)),
            compiler_params=SMALL,
            cost_estimate=cost(m, 1000),
            name=f"y{start}",
        )(s, *((b, f) if swapped else (f, b)))

    def z_sweep(start, m, t, f, b, out):
        w = m * NY
        first = out is None
        near = pl.BlockSpec(memory_space=pltpu.VMEM)
        far = pl.BlockSpec(memory_space=pl.ANY)
        kernel = functools.partial(z_kernel, start, m)
        return pl.pallas_call(
            (lambda t, b, f, *rest: kernel(t, b, f, None, *rest)) if first else kernel,
            in_specs=[near] * 3 + [far] * (not first),
            out_specs=far,
            out_shape=shape(5, NZ, TILES * NY, 128),
            scratch_shapes=[pltpu.VMEM((5, NZ, w, 128), F32), pltpu.SemaphoreType.DMA((w // 8,))],
            input_output_aliases={} if first else {3: 0},
            compiler_params=SMALL,
            cost_estimate=cost(m, 1000),
            name=f"z{start}",
        )(t, b, f, *([] if first else [out]))

    y_in = []
    for start, m in chunks:
        s, f, b = x_sweep(start, m)
        y_in.append((s, lax.ppermute(f, "row", across), lax.ppermute(b, "row", inside)))
    z_in = []
    for (start, m), args in zip(chunks, y_in):
        t, f, b = y_sweep(start, m, *args)
        z_in.append((t, lax.ppermute(b, "col", inside), lax.ppermute(f, "col", across)))
    out = None
    for (start, m), (t, b, f) in zip(chunks, z_in):
        out = z_sweep(start, m, t, f, b, out)
    return unrows(out)


def solution(mesh):
    placed = (P("col", "row", None), P(None, "col", "row", None), P("col", "row", None))
    return jax.shard_map(
        local, mesh=mesh, in_specs=placed, out_specs=P(None, "col", "row", None), check_vma=False
    )
```

```python
import functools

import jax
import jax.numpy as jnp
from jax import lax
from jax.experimental import pallas as pl
from jax.experimental.pallas import tpu as pltpu
from jax.sharding import PartitionSpec as P

RIEMANN_ITERS = 3
GAMMA = 1.4
GM1 = 0.4
SHOCK = (GAMMA + 1.0) / (2.0 * GAMMA)
DTDX = 0.03
PRESSURE_FLOOR = 0.05
STAR_FLOOR = 0.1

NX, NY, NZ = 1024, 4, 8
TILES = NX // 128
HALO = 3
F32 = jnp.float32


def face_values(q0, q1, q2, q3):
    face = 7.0 / 12.0 * (q1 + q2) - 1.0 / 12.0 * (q0 + q3)
    return jnp.minimum(jnp.maximum(face, jnp.minimum(q1, q2)), jnp.maximum(q1, q2))


def cell_edges(q, face_left, face_right):
    dr = face_right - q
    dl = face_left - q
    br = 2.0 * jnp.abs(dr)
    bl = 2.0 * jnp.abs(dl)
    right = q + jnp.minimum(jnp.maximum(dr, -bl), bl)
    left = q + jnp.minimum(jnp.maximum(dl, -br), br)
    return left, right


def root(x):
    return x * lax.rsqrt(x)


def inverse(x):
    return 1.0 / x


def riemann(left, right):
    rl, ul, vl, wl, pl_ = left
    rr, ur, vr, wr, pr = right
    al = GAMMA * rl
    ar = GAMMA * rr
    cl = root(al * pl_)
    cr = root(ar * pr)
    jump = ul - ur
    floor = STAR_FLOOR * jnp.minimum(pl_, pr)
    sl = SHOCK * al
    sr = SHOCK * ar
    bl = (1.0 - SHOCK) * al * pl_
    br = (1.0 - SHOCK) * ar * pr

    def star(a, b):
        return jnp.maximum((b * (pl_ + a * jump) + a * pr) * inverse(a + b), floor)

    p = star(cl, cr)
    for _ in range(RIEMANN_ITERS):
        p = star(root(bl + sl * p), root(br + sr * p))
    a = root(bl + sl * p)
    b = root(br + sr * p)
    u = (a * ul + b * ur + (pl_ - pr)) * inverse(a + b)
    up = u > 0.0
    r = jnp.where(up, rl, rr)
    v = jnp.where(up, vl, vr)
    w = jnp.where(up, wl, wr)
    pu = jnp.where(up, pl_, pr)
    m = r * u
    energy = (1.0 / GM1) * pu + 0.5 * r * (u * u + v * v + w * w)
    return m, m * u + p, m * v, m * w, u * (energy + p)


def primitives(state, normal):
    rho = state[0]
    inv = inverse(rho)
    mom = [state[c] for c in normal]
    vel = [m * inv for m in mom]
    kinetic = 0.5 * (mom[0] * vel[0] + mom[1] * vel[1] + mom[2] * vel[2])
    pressure = jnp.maximum(GM1 * (state[4] - kinetic), PRESSURE_FLOOR)
    return [rho] + vel + [pressure]


def line_change(prims, cells):
    left, right = [], []
    for q in prims:
        n = q.shape[0]
        face = face_values(q[0 : n - 3], q[1 : n - 2], q[2 : n - 1], q[3:n])
        lo, hi = cell_edges(q[2 : n - 2], face[: n - 4], face[1:])
        left.append(hi[: cells + 1])
        right.append(lo[1:])
    flux = riemann(left, right)
    return [DTDX * (f[1:] - f[:-1]) for f in flux]


def x_kernel(start, m, q_ref, s_ref, f_ref, b_ref, work, done):
    rows_per = NY * NZ
    lanes = m * rows_per
    lane = lax.broadcasted_iota(jnp.int32, (8, lanes), 1)

    def tile(c, t):
        at = (start + t) % TILES * NY
        return [q_ref[c, pl.ds(at + y, NZ, stride=TILES * NY), :] for y in range(NY)]

    for c in range(5):
        own = jnp.concatenate([r for t in range(m) for r in tile(c, t)], axis=0).T
        before, behind = tile(c, -1), tile(c, m)
        edge = jnp.concatenate(before * (m - 1) + behind, axis=0).T
        work[c, 8:136] = own
        work[c, 0:8] = jnp.where(lane < rows_per, edge[120:], pltpu.roll(own[120:], rows_per, axis=1))
        work[c, 136:144] = jnp.where(lane >= lanes - rows_per, edge[:8], pltpu.roll(own[:8], lanes - rows_per, axis=1))
    cells = 16
    prims, faces, edges, flux = [], [], [], None
    for k in range(cells + 2 * HALO):
        prims.append([work[c, pl.ds(8 + k - HALO, 8, stride=cells), :] for c in range(5)])
        if k < 3:
            continue
        faces.append([face_values(*(prims[k - 3 + i][c] for i in range(4))) for c in range(5)])
        if k < 4:
            continue
        edges.append([cell_edges(prims[k - 2][c], faces[-2][c], faces[-1][c]) for c in range(5)])
        if k < 5:
            continue
        now = riemann([e[1] for e in edges[-2]], [e[0] for e in edges[-1]])
        if k > 5:
            rho, u, v, w, p = prims[k - 3]
            kinetic = 0.5 * rho * (u * u + v * v + w * w)
            state = (rho, rho * u, rho * v, rho * w, (1.0 / GM1) * p + kinetic)
            for c in range(5):
                done[c, pl.ds(k - 6, 8, stride=cells), :] = state[c] - DTDX * (now[c] - flux[c])
        flux = now
    for c in range(5):
        back = done[c].T
        for t in range(m):
            for y in range(NY):
                s_ref[c, y, t] = back[(t * NY + y) * NZ : (t * NY + y + 1) * NZ]
    odd = lax.rem(lax.axis_index("row"), 2)
    f_ref[...] = s_ref[:, pl.ds(odd, HALO)]
    b_ref[...] = s_ref[:, pl.ds(1 - odd, HALO)]


def y_kernel(per, s_ref, f_in, b_in, t_ref, f_ref, b_ref):
    odd = lax.rem(lax.axis_index("row"), 2) == 1
    for t in range(per):
        full = [
            jnp.concatenate(
                [
                    jnp.where(odd, b_in[c, :, t], f_in[c, :, t]),
                    s_ref[c, :, t],
                    jnp.where(odd, f_in[c, :, t], b_in[c, :, t]),
                ],
                axis=0,
            )
            for c in range(5)
        ]
        change = line_change(primitives(full, (2, 1, 3)), NY)
        for c, k in enumerate((0, 2, 1, 3, 4)):
            new = full[c][HALO : HALO + NY] - change[k]
            for y in range(NY):
                t_ref[c, pl.ds(t * NY + y, NZ, stride=per * NY), :] = new[y]
    width = per * NY
    odd = lax.rem(lax.axis_index("col"), 2)
    for c in range(5):
        f_ref[c] = t_ref[c, pl.ds(pl.multiple_of(odd * (NZ - HALO) * width, 8), HALO * width)]
        b_ref[c] = t_ref[c, pl.ds(pl.multiple_of((1 - odd) * (NZ - HALO) * width, 8), HALO * width)]


def z_kernel(start, per, t_ref, b_in, f_in, _, o_hbm, o_ref, sems):
    width = per * NY
    odd = lax.rem(lax.axis_index("col"), 2) == 1

    def halo(even_ref, odd_ref, c, z, r):
        at = slice(z * width + r, z * width + r + 8)
        return jnp.where(odd, odd_ref[c, at], even_ref[c, at])

    copies = []
    for i, r in enumerate(range(0, width, 8)):
        full = [
            jnp.stack(
                [halo(f_in, b_in, c, z, r) for z in range(HALO)]
                + [t_ref[c, z * width + r : z * width + r + 8] for z in range(NZ)]
                + [halo(b_in, f_in, c, z, r) for z in range(HALO)]
            )
            for c in range(5)
        ]
        change = line_change(primitives(full, (3, 1, 2)), NZ)
        for c, k in enumerate((0, 2, 3, 1, 4)):
            new = full[c][HALO : HALO + NZ] - change[k]
            for z in range(NZ):
                o_ref[c, z, r : r + 8] = new[z]
        copies.append(
            pltpu.make_async_copy(
                o_ref.at[:, :, r : r + 8], o_hbm.at[:, :, start * NY + r : start * NY + r + 8], sems.at[i]
            )
        )
        copies[-1].start()
    for copy in copies:
        copy.wait()


def z_inner(per, t_ref, q_ref, mid_ref):
    for r in range(0, per * NY, 8):
        at = slice(r, r + 8)
        own = [[t_ref[c, z * per * NY + r : z * per * NY + r + 8] for c in range(5)] for z in range(NZ)]
        q = [primitives(u, (3, 1, 2)) for u in own]
        face = {k: [face_values(*(q[k + i][c] for i in (-1, 0, 1, 2))) for c in range(5)] for k in range(1, 6)}
        edge = {k: [cell_edges(q[k][c], face[k - 1][c], face[k][c]) for c in range(5)] for k in range(2, 6)}
        flux = [riemann([e[1] for e in edge[k]], [e[0] for e in edge[k + 1]]) for k in (2, 3, 4)]
        kept = [face[1], face[5], [e[0] for e in edge[2]], [e[1] for e in edge[5]]] + flux
        for c in range(5):
            for z in range(NZ):
                q_ref[c, z, at] = q[z][c]
            for i, v in enumerate(kept):
                mid_ref[c, i, at] = v[c]


def z_outer(start, per, t_ref, q_ref, mid_ref, b_in, f_in, _, o_hbm, o_ref, sems):
    width = per * NY
    odd = lax.rem(lax.axis_index("col"), 2) == 1
    copies = []
    for i, r in enumerate(range(0, width, 8)):
        at = slice(r, r + 8)

        def halo(even_ref, odd_ref, z):
            rows_at = slice(z * width + r, z * width + r + 8)
            picked = [jnp.where(odd, odd_ref[c, rows_at], even_ref[c, rows_at]) for c in range(5)]
            return primitives(picked, (3, 1, 2))

        q = {z: [q_ref[c, z, at] for c in range(5)] for z in range(NZ)}
        q.update({z - HALO: halo(f_in, b_in, z) for z in range(HALO)})
        q.update({z + NZ: halo(b_in, f_in, z) for z in range(HALO)})
        kept = [[mid_ref[c, j, at] for c in range(5)] for j in range(7)]
        face = {1: kept[0], 5: kept[1]}
        for k in (-2, -1, 0, 6, 7, 8):
            face[k] = [face_values(*(q[k + j][c] for j in (-1, 0, 1, 2))) for c in range(5)]
        low, high = {2: kept[2]}, {5: kept[3]}
        for k in (-1, 0, 1, 6, 7, 8):
            both = [cell_edges(q[k][c], face[k - 1][c], face[k][c]) for c in range(5)]
            low[k], high[k] = [e[0] for e in both], [e[1] for e in both]
        flux = {2: kept[4], 3: kept[5], 4: kept[6]}
        for k in (-1, 0, 1, 5, 6, 7):
            flux[k] = riemann(high[k], low[k + 1])
        for z in range(NZ):
            for k, c in enumerate((0, 3, 1, 2, 4)):
                old = t_ref[c, z * width + r : z * width + r + 8]
                o_ref[c, z, at] = old - DTDX * (flux[z][k] - flux[z - 1][k])
        rows_out = slice(start * NY + r, start * NY + r + 8)
        copies.append(pltpu.make_async_copy(o_ref.at[:, :, at], o_hbm.at[:, :, rows_out], sems.at[i]))
        copies[-1].start()
    for copy in copies:
        copy.wait()


def rows(a):
    lead = a.shape[:-3]
    a = jnp.swapaxes(a.reshape(*lead, NZ, NY, TILES, 128), -2, -3)
    return a.reshape(*lead, NZ * TILES * NY, 128)


def unrows(a):
    a = jnp.swapaxes(a.reshape(5, NZ, TILES, NY, 128), -2, -3)
    return a.reshape(5, NZ, NY, NX)


def cost(m, ops):
    cells = NZ * NY * 128 * m
    return pl.CostEstimate(flops=ops * cells, bytes_accessed=80 * cells, transcendentals=12 * cells)


def shape(*s):
    return jax.ShapeDtypeStruct(s, F32)


SMALL = pltpu.CompilerParams(vmem_limit_bytes=12 << 20)


CUTS = (0, 4, 8)


def local(density, velocity, pressure):
    n = lax.axis_size("row")
    inside = [(i, i ^ 1) for i in range(n)]
    across = [(i, (i + 1 if i % 2 else i - 1) % n) for i in range(n)]
    chunks = [(a, b - a) for a, b in zip(CUTS, CUTS[1:])]
    prims = jnp.concatenate([rows(density)[None], rows(velocity), rows(pressure)[None]])

    def x_sweep(start, m):
        return pl.pallas_call(
            functools.partial(x_kernel, start, m),
            out_shape=(shape(5, NY, m, NZ, 128), shape(5, HALO, m, NZ, 128), shape(5, HALO, m, NZ, 128)),
            compiler_params=SMALL,
            scratch_shapes=[pltpu.VMEM((5, 144, m * NY * NZ), F32), pltpu.VMEM((5, 128, m * NY * NZ), F32)],
            cost_estimate=cost(m, 1500),
            name=f"x{start}",
        )(prims)

    def y_sweep(start, m, s, f, b):
        w = m * NY
        kernel = functools.partial(y_kernel, m)
        swapped = start > 0
        return pl.pallas_call(
            (lambda s, b, f, *rest: kernel(s, f, b, *rest)) if swapped else kernel,
            out_shape=(shape(5, NZ * w, 128), shape(5, HALO * w, 128), shape(5, HALO * w, 128)),
            compiler_params=SMALL,
            cost_estimate=cost(m, 1000),
            name=f"y{start}",
        )(s, *((b, f) if swapped else (f, b)))

    def z_sweep(start, m, t, f, b, out):
        w = m * NY
        first = out is None
        near = pl.BlockSpec(memory_space=pltpu.VMEM)
        far = pl.BlockSpec(memory_space=pl.ANY)
        kernel = functools.partial(z_kernel, start, m)
        return pl.pallas_call(
            (lambda t, b, f, *rest: kernel(t, b, f, None, *rest)) if first else kernel,
            in_specs=[near] * 3 + [far] * (not first),
            out_specs=far,
            out_shape=shape(5, NZ, TILES * NY, 128),
            scratch_shapes=[pltpu.VMEM((5, NZ, w, 128), F32), pltpu.SemaphoreType.DMA((w // 8,))],
            input_output_aliases={} if first else {3: 0},
            compiler_params=SMALL,
            cost_estimate=cost(m, 1000),
            name=f"z{start}",
        )(t, b, f, *([] if first else [out]))

    def z_split(start, m, t, f, b, out):
        w = m * NY
        near = pl.BlockSpec(memory_space=pltpu.VMEM)
        far = pl.BlockSpec(memory_space=pl.ANY)
        q, mid = pl.pallas_call(
            functools.partial(z_inner, m),
            out_shape=(shape(5, NZ, w, 128), shape(5, 7, w, 128)),
            compiler_params=SMALL,
            cost_estimate=cost(m, 500),
            name=f"inner{start}",
        )(t)
        return pl.pallas_call(
            functools.partial(z_outer, start, m),
            in_specs=[near] * 5 + [far],
            out_specs=far,
            out_shape=shape(5, NZ, TILES * NY, 128),
            scratch_shapes=[pltpu.VMEM((5, NZ, w, 128), F32), pltpu.SemaphoreType.DMA((w // 8,))],
            input_output_aliases={5: 0},
            compiler_params=SMALL,
            cost_estimate=cost(m, 700),
            name=f"z{start}",
        )(t, q, mid, b, f, out)

    y_in = []
    for start, m in chunks:
        s, f, b = x_sweep(start, m)
        y_in.append((s, lax.ppermute(f, "row", across), lax.ppermute(b, "row", inside)))
    z_in = []
    for (start, m), args in zip(chunks, y_in):
        t, f, b = y_sweep(start, m, *args)
        z_in.append((t, lax.ppermute(b, "col", inside), lax.ppermute(f, "col", across)))
    out = None
    for (start, m), (t, b, f) in zip(chunks, z_in):
        out = (z_split if start else z_sweep)(start, m, t, f, b, out)
    return unrows(out)


def solution(mesh):
    placed = (P("col", "row", None), P(None, "col", "row", None), P("col", "row", None))
    return jax.shard_map(
        local, mesh=mesh, in_specs=placed, out_specs=P(None, "col", "row", None), check_vma=False
    )
```

```python
import functools

import jax
import jax.numpy as jnp
from jax import lax
from jax.experimental import pallas as pl
from jax.experimental.pallas import tpu as pltpu
from jax.sharding import PartitionSpec as P

RIEMANN_ITERS = 3
GAMMA = 1.4
GM1 = 0.4
SHOCK = (GAMMA + 1.0) / (2.0 * GAMMA)
DTDX = 0.03
PRESSURE_FLOOR = 0.05
STAR_FLOOR = 0.1

NX, NY, NZ = 1024, 4, 8
TILES = NX // 128
HALO = 3
F32 = jnp.float32


def face_values(q0, q1, q2, q3):
    face = 7.0 / 12.0 * (q1 + q2) - 1.0 / 12.0 * (q0 + q3)
    return jnp.minimum(jnp.maximum(face, jnp.minimum(q1, q2)), jnp.maximum(q1, q2))


def cell_edges(q, face_left, face_right):
    dr = face_right - q
    dl = face_left - q
    br = 2.0 * jnp.abs(dr)
    bl = 2.0 * jnp.abs(dl)
    right = q + jnp.minimum(jnp.maximum(dr, -bl), bl)
    left = q + jnp.minimum(jnp.maximum(dl, -br), br)
    return left, right


def root(x):
    return x * lax.rsqrt(x)


def inverse(x):
    return 1.0 / x


def riemann(left, right):
    rl, ul, vl, wl, pl_ = left
    rr, ur, vr, wr, pr = right
    al = GAMMA * rl
    ar = GAMMA * rr
    cl = root(al * pl_)
    cr = root(ar * pr)
    jump = ul - ur
    floor = STAR_FLOOR * jnp.minimum(pl_, pr)
    sl = SHOCK * al
    sr = SHOCK * ar
    bl = (1.0 - SHOCK) * al * pl_
    br = (1.0 - SHOCK) * ar * pr

    def star(a, b):
        return jnp.maximum((b * (pl_ + a * jump) + a * pr) * inverse(a + b), floor)

    p = star(cl, cr)
    for _ in range(RIEMANN_ITERS):
        p = star(root(bl + sl * p), root(br + sr * p))
    a = root(bl + sl * p)
    b = root(br + sr * p)
    u = (a * ul + b * ur + (pl_ - pr)) * inverse(a + b)
    up = u > 0.0
    r = jnp.where(up, rl, rr)
    v = jnp.where(up, vl, vr)
    w = jnp.where(up, wl, wr)
    pu = jnp.where(up, pl_, pr)
    m = r * u
    energy = (1.0 / GM1) * pu + 0.5 * r * (u * u + v * v + w * w)
    return m, m * u + p, m * v, m * w, u * (energy + p)


def primitives(state, normal):
    rho = state[0]
    inv = inverse(rho)
    mom = [state[c] for c in normal]
    vel = [m * inv for m in mom]
    kinetic = 0.5 * (mom[0] * vel[0] + mom[1] * vel[1] + mom[2] * vel[2])
    pressure = jnp.maximum(GM1 * (state[4] - kinetic), PRESSURE_FLOOR)
    return [rho] + vel + [pressure]


def line_change(prims, cells):
    left, right = [], []
    for q in prims:
        n = q.shape[0]
        face = face_values(q[0 : n - 3], q[1 : n - 2], q[2 : n - 1], q[3:n])
        lo, hi = cell_edges(q[2 : n - 2], face[: n - 4], face[1:])
        left.append(hi[: cells + 1])
        right.append(lo[1:])
    flux = riemann(left, right)
    return [DTDX * (f[1:] - f[:-1]) for f in flux]


def x_kernel(start, m, q_ref, s_ref, f_ref, b_ref, work, done):
    rows_per = NY * NZ
    lanes = m * rows_per
    lane = lax.broadcasted_iota(jnp.int32, (8, lanes), 1)

    def tile(c, t):
        at = (start + t) % TILES * NY
        return [q_ref[c, pl.ds(at + y, NZ, stride=TILES * NY), :] for y in range(NY)]

    for c in range(5):
        own = jnp.concatenate([r for t in range(m) for r in tile(c, t)], axis=0).T
        before, behind = tile(c, -1), tile(c, m)
        edge = jnp.concatenate(before * (m - 1) + behind, axis=0).T
        work[c, 8:136] = own
        work[c, 0:8] = jnp.where(lane < rows_per, edge[120:], pltpu.roll(own[120:], rows_per, axis=1))
        work[c, 136:144] = jnp.where(lane >= lanes - rows_per, edge[:8], pltpu.roll(own[:8], lanes - rows_per, axis=1))
    cells = 16
    prims, faces, edges, flux = [], [], [], None
    for k in range(cells + 2 * HALO):
        prims.append([work[c, pl.ds(8 + k - HALO, 8, stride=cells), :] for c in range(5)])
        if k < 3:
            continue
        faces.append([face_values(*(prims[k - 3 + i][c] for i in range(4))) for c in range(5)])
        if k < 4:
            continue
        edges.append([cell_edges(prims[k - 2][c], faces[-2][c], faces[-1][c]) for c in range(5)])
        if k < 5:
            continue
        now = riemann([e[1] for e in edges[-2]], [e[0] for e in edges[-1]])
        if k > 5:
            rho, u, v, w, p = prims[k - 3]
            kinetic = 0.5 * rho * (u * u + v * v + w * w)
            state = (rho, rho * u, rho * v, rho * w, (1.0 / GM1) * p + kinetic)
            for c in range(5):
                done[c, pl.ds(k - 6, 8, stride=cells), :] = state[c] - DTDX * (now[c] - flux[c])
        flux = now
    for c in range(5):
        back = done[c].T
        for t in range(m):
            for y in range(NY):
                s_ref[c, y, t] = back[(t * NY + y) * NZ : (t * NY + y + 1) * NZ]
    odd = lax.rem(lax.axis_index("row"), 2)
    f_ref[...] = s_ref[:, pl.ds(odd, HALO)]
    b_ref[...] = s_ref[:, pl.ds(1 - odd, HALO)]


def y_kernel(per, s_ref, f_in, b_in, t_ref, f_ref, b_ref):
    odd = lax.rem(lax.axis_index("row"), 2) == 1
    for t in range(per):
        full = [
            jnp.concatenate(
                [
                    jnp.where(odd, b_in[c, :, t], f_in[c, :, t]),
                    s_ref[c, :, t],
                    jnp.where(odd, f_in[c, :, t], b_in[c, :, t]),
                ],
                axis=0,
            )
            for c in range(5)
        ]
        change = line_change(primitives(full, (2, 1, 3)), NY)
        for c, k in enumerate((0, 2, 1, 3, 4)):
            new = full[c][HALO : HALO + NY] - change[k]
            for y in range(NY):
                t_ref[c, pl.ds(t * NY + y, NZ, stride=per * NY), :] = new[y]
    width = per * NY
    odd = lax.rem(lax.axis_index("col"), 2)
    for c in range(5):
        f_ref[c] = t_ref[c, pl.ds(pl.multiple_of(odd * (NZ - HALO) * width, 8), HALO * width)]
        b_ref[c] = t_ref[c, pl.ds(pl.multiple_of((1 - odd) * (NZ - HALO) * width, 8), HALO * width)]


def z_inner(per, t_ref, q_ref, mid_ref):
    for r in range(0, per * NY, 8):
        at = slice(r, r + 8)
        own = [[t_ref[c, z * per * NY + r : z * per * NY + r + 8] for c in range(5)] for z in range(NZ)]
        q = [primitives(u, (3, 1, 2)) for u in own]
        face = {k: [face_values(*(q[k + i][c] for i in (-1, 0, 1, 2))) for c in range(5)] for k in range(1, 6)}
        edge = {k: [cell_edges(q[k][c], face[k - 1][c], face[k][c]) for c in range(5)] for k in range(2, 6)}
        flux = [riemann([e[1] for e in edge[k]], [e[0] for e in edge[k + 1]]) for k in (2, 3, 4)]
        kept = [face[1], face[5], [e[0] for e in edge[2]], [e[1] for e in edge[5]]] + flux
        for c in range(5):
            for z in range(NZ):
                q_ref[c, z, at] = q[z][c]
            for i, v in enumerate(kept):
                mid_ref[c, i, at] = v[c]


def z_outer(start, per, t_ref, q_ref, mid_ref, b_in, f_in, _, o_hbm, o_ref, sems):
    width = per * NY
    odd = lax.rem(lax.axis_index("col"), 2) == 1
    copies = []
    for i, r in enumerate(range(0, width, 8)):
        at = slice(r, r + 8)

        def halo(even_ref, odd_ref, z):
            rows_at = slice(z * width + r, z * width + r + 8)
            picked = [jnp.where(odd, odd_ref[c, rows_at], even_ref[c, rows_at]) for c in range(5)]
            return primitives(picked, (3, 1, 2))

        q = {z: [q_ref[c, z, at] for c in range(5)] for z in range(NZ)}
        q.update({z - HALO: halo(f_in, b_in, z) for z in range(HALO)})
        q.update({z + NZ: halo(b_in, f_in, z) for z in range(HALO)})
        kept = [[mid_ref[c, j, at] for c in range(5)] for j in range(7)]
        face = {1: kept[0], 5: kept[1]}
        for k in (-2, -1, 0, 6, 7, 8):
            face[k] = [face_values(*(q[k + j][c] for j in (-1, 0, 1, 2))) for c in range(5)]
        low, high = {2: kept[2]}, {5: kept[3]}
        for k in (-1, 0, 1, 6, 7, 8):
            both = [cell_edges(q[k][c], face[k - 1][c], face[k][c]) for c in range(5)]
            low[k], high[k] = [e[0] for e in both], [e[1] for e in both]
        flux = {2: kept[4], 3: kept[5], 4: kept[6]}
        for k in (-1, 0, 1, 5, 6, 7):
            flux[k] = riemann(high[k], low[k + 1])
        for z in range(NZ):
            for k, c in enumerate((0, 3, 1, 2, 4)):
                old = t_ref[c, z * width + r : z * width + r + 8]
                o_ref[c, z, at] = old - DTDX * (flux[z][k] - flux[z - 1][k])
        rows_out = slice(start * NY + r, start * NY + r + 8)
        copies.append(pltpu.make_async_copy(o_ref.at[:, :, at], o_hbm.at[:, :, rows_out], sems.at[i]))
        copies[-1].start()
    for copy in copies:
        copy.wait()


def rows(a):
    lead = a.shape[:-3]
    a = jnp.swapaxes(a.reshape(*lead, NZ, NY, TILES, 128), -2, -3)
    return a.reshape(*lead, NZ * TILES * NY, 128)


def unrows(a):
    a = jnp.swapaxes(a.reshape(5, NZ, TILES, NY, 128), -2, -3)
    return a.reshape(5, NZ, NY, NX)


def cost(m, ops):
    cells = NZ * NY * 128 * m
    return pl.CostEstimate(flops=ops * cells, bytes_accessed=80 * cells, transcendentals=12 * cells)


def shape(*s):
    return jax.ShapeDtypeStruct(s, F32)


SMALL = pltpu.CompilerParams(vmem_limit_bytes=12 << 20)


CUTS = (0, 4, 8)


def local(density, velocity, pressure):
    n = lax.axis_size("row")
    inside = [(i, i ^ 1) for i in range(n)]
    across = [(i, (i + 1 if i % 2 else i - 1) % n) for i in range(n)]
    chunks = [(a, b - a) for a, b in zip(CUTS, CUTS[1:])]
    prims = jnp.concatenate([rows(density)[None], rows(velocity), rows(pressure)[None]])

    def x_sweep(start, m):
        return pl.pallas_call(
            functools.partial(x_kernel, start, m),
            out_shape=(shape(5, NY, m, NZ, 128), shape(5, HALO, m, NZ, 128), shape(5, HALO, m, NZ, 128)),
            compiler_params=SMALL,
            scratch_shapes=[pltpu.VMEM((5, 144, m * NY * NZ), F32), pltpu.VMEM((5, 128, m * NY * NZ), F32)],
            cost_estimate=cost(m, 1500),
            name=f"x{start}",
        )(prims)

    def y_sweep(start, m, s, f, b):
        w = m * NY
        kernel = functools.partial(y_kernel, m)
        swapped = start > 0
        return pl.pallas_call(
            (lambda s, b, f, *rest: kernel(s, f, b, *rest)) if swapped else kernel,
            out_shape=(shape(5, NZ * w, 128), shape(5, HALO * w, 128), shape(5, HALO * w, 128)),
            compiler_params=SMALL,
            cost_estimate=cost(m, 1000),
            name=f"y{start}",
        )(s, *((b, f) if swapped else (f, b)))

    def z_split(start, m, t, f, b, out):
        w = m * NY
        near = pl.BlockSpec(memory_space=pltpu.VMEM)
        far = pl.BlockSpec(memory_space=pl.ANY)
        q, mid = pl.pallas_call(
            functools.partial(z_inner, m),
            out_shape=(shape(5, NZ, w, 128), shape(5, 7, w, 128)),
            compiler_params=SMALL,
            cost_estimate=cost(m, 500),
            name=f"inner{start}",
        )(t)
        first = out is None
        kernel = functools.partial(z_outer, start, m)
        return pl.pallas_call(
            (lambda t, q, mid, b, f, *rest: kernel(t, q, mid, b, f, None, *rest)) if first else kernel,
            in_specs=[near] * 5 + [far] * (not first),
            out_specs=far,
            out_shape=shape(5, NZ, TILES * NY, 128),
            scratch_shapes=[pltpu.VMEM((5, NZ, w, 128), F32), pltpu.SemaphoreType.DMA((w // 8,))],
            input_output_aliases={} if first else {5: 0},
            compiler_params=SMALL,
            cost_estimate=cost(m, 700),
            name=f"z{start}",
        )(t, q, mid, b, f, *([] if first else [out]))

    y_in = []
    for start, m in chunks:
        s, f, b = x_sweep(start, m)
        y_in.append((s, lax.ppermute(f, "row", across), lax.ppermute(b, "row", inside)))
    z_in = []
    for (start, m), args in zip(chunks, y_in):
        t, f, b = y_sweep(start, m, *args)
        z_in.append((t, lax.ppermute(b, "col", inside), lax.ppermute(f, "col", across)))
    out = None
    for (start, m), (t, b, f) in zip(chunks, z_in):
        out = z_split(start, m, t, f, b, out)
    return unrows(out)


def solution(mesh):
    placed = (P("col", "row", None), P(None, "col", "row", None), P("col", "row", None))
    return jax.shard_map(
        local, mesh=mesh, in_specs=placed, out_specs=P(None, "col", "row", None), check_vma=False
    )
```
